256 devices in a mesh: row: 32 (over z, x), col: 8 (over y, core).
Axes of the slice: x: 4, y: 4, z: 8, core: 2. Of those that a mesh axis runs over, the one named last changes fastest.
Arguments:
- block_cost: bfloat16 [512, 16, 256, 256], P('row', 'col'), may hold values from 0 to 15, as said below
- candidates: int32 [512, 16], P('row', 'col'), may hold values from 0 to 255, all different within a row
- source_logmass: float32 [512, 256], P('row'), may hold values from -4 to 4
- target_logmass: float32 [256, 256], replicated, may hold values from -4 to 4
Outputs:
- source_potential: float32 [512, 256], P('row')
- target_potential: float32 [256, 256], replicated
The draws below stay inside these ranges and needn't reach their ends.
Inputs may be any that keep to these rules, and one draw needn't show every extreme that they name: Each row of candidates names 16 distinct target blocks, and every target block is named by some row. `block_cost`: costs are nonnegative.
All inputs are finite; a program needn't handle non-finite values.
Results may differ from the reference program's by a relative error of at most 0.0003.
Values sent between devices are 32-bit elements; how exact they have to be, the bound alone decides.
A program may use at most 256 MiB of HBM per device.

```python
import jax
import jax.numpy as jnp
from jax import lax

BS = 256
K = 16
ITERS = 2
RB = 512
CB = 256


def draw_block_cost(key, part):
    first = jax.random.fold_in(key, 0)
    values = jax.random.uniform(first, (RB, K, BS, BS), jnp.float32, 0.0, 4.0)
    return values.astype(jnp.bfloat16)


def steps_of(stream_key, dims, pieces, low, high):
    loudness, own = 1.0, jax.random.fold_in(stream_key, 6)
    for dim, shards_of in pieces:
        steps = jnp.exp(jax.random.uniform(jax.random.fold_in(own, dim), (shards_of,), jnp.float32, low / len(pieces), high / len(pieces)))
        loudness = loudness * jnp.repeat(steps, dims[dim] // shards_of).reshape([-1 if axis == dim else 1 for axis in range(len(dims))])
    return loudness


def different_ones(rng, rows, count, top, lift):
    ranking = jax.random.permutation(jax.random.fold_in(rng, 1), count)
    boost = ranking
    for power in range(3):
        boost = boost * boost // count
    boost = boost * lift // count
    tickets = jax.random.randint(jax.random.fold_in(rng, 2), (rows, count), 0, 4096) + boost
    fixed_rows = jax.random.permutation(jax.random.fold_in(rng, 3), rows)[jnp.arange(count) % rows]
    tickets = jnp.where(jnp.arange(rows)[:, None] == fixed_rows[None, :], 1 << 14, tickets)
    merit = tickets * count + jnp.arange(count)
    return lax.top_k(merit.astype(jnp.int32), top)[1].astype(jnp.int32)


def setup_inputs(seed: int = 0) -> dict:
    key_of = jax.random.split(jax.random.key(seed), 5)
    return {
        "block_cost": draw_block_cost(jax.random.fold_in(key_of[4], 71), 0),
        "candidates": different_ones(key_of[1], RB, CB, K, 1024),
        "source_logmass": jnp.clip(jax.random.uniform(key_of[2], (RB, BS), jnp.float32, -4.0, 4.0) * steps_of(key_of[2], (RB, BS), ((0, 32),), -0.4, 0.0), -4.0, 4.0),
        "target_logmass": jnp.clip(jax.random.uniform(key_of[3], (CB, BS), jnp.float32, -4.0, 4.0), -4.0, 4.0),
    }


EPS = 0.05
LOWEST = -1.0e30


def reference(block_cost, candidates, source_logmass, target_logmass):
    target_pot = jnp.zeros((CB, BS), jnp.float32)
    source_pot = jnp.zeros((RB, BS), jnp.float32)
    flat_ids = candidates.reshape(-1).astype(jnp.int32)
    for step_index in range(ITERS):
        nearby = target_pot[candidates]

        def row_block(operands):
            costs, potential = operands
            scores = (potential[:, None, :] - costs.astype(jnp.float32)) / EPS
            highest = jnp.max(scores, axis=(0, 2))
            totals = jnp.sum(jnp.exp(scores - highest[None, :, None]), axis=(0, 2))
            return highest + jnp.log(totals)

        source_pot = EPS * source_logmass - EPS * lax.map(row_block, (block_cost, nearby))

        def col_block(operands):
            costs, potential = operands
            scores = (potential[None, :, None] - costs.astype(jnp.float32)) / EPS
            highest = jnp.max(scores, axis=1)
            totals = jnp.sum(jnp.exp(scores - highest[:, None, :]), axis=1)
            return highest, totals

        col_high, col_total = lax.map(col_block, (block_cost, source_pot))
        col_high = col_high.reshape(-1, BS)
        col_total = col_total.reshape(-1, BS)
        peaks = jnp.full((CB, BS), LOWEST, jnp.float32).at[flat_ids].max(col_high)
        masses = jnp.zeros((CB, BS), jnp.float32).at[flat_ids].add(col_total * jnp.exp(col_high - peaks[flat_ids]))
        target_pot = EPS * target_logmass - EPS * (peaks + jnp.log(masses))
    return source_pot, target_pot
```

```python
import functools
import math

import jax
import jax.numpy as jnp
from jax import lax
from jax.experimental import pallas as pl
from jax.experimental.pallas import tpu as pltpu
from jax.sharding import PartitionSpec as P

ITERS = 2
EPS = 0.05
LOG2E = math.log2(math.e)
SCALE = LOG2E / EPS
UNSCALE = EPS / LOG2E
LOWEST = -1e30
MESH = pl.DeviceIdType.MESH
NX, NY, NZ, NC = 4, 4, 8, 2
PLANE = NX * NY * NC
NCOL = NY * NC
ROWS, KK, BS = 16, 2, 256
ENT = ROWS * KK
SLAB = 64
GROUP = 8 // KK
HIGHEST = lax.Precision.HIGHEST


def lse2(parts):
    top = jnp.max(parts, axis=0)
    return top + jnp.log2(jnp.sum(jnp.exp2(parts - top[None]), axis=0))


def body(
    cand_ref, cost_hbm, slm_ref, tlm_hbm, src_out, tgt_out,
    cost, c2, tlm, xm, xs, st, ment, sent, onehot, same,
    a_src, a_recv, dense, r_recv, z_src, z_recv, t_src, t_recv,
    in_sem, a_ss, a_rs, r_ss, r_rs, z_ss, z_rs, t_ss, t_rs,
):
    row, col = lax.axis_index("row"), lax.axis_index("col")
    z, x = row // NX, row % NX
    y, co = col // NC, col % NC
    me = x * NCOL + col

    def plane_peer(s):
        px = (x + s // NCOL) % NX
        pc = ((y + (s // NC) % NY) % NY) * NC + (co + s) % NC
        return (z * NX + px, pc), px * NCOL + pc

    def z_peer(s):
        return (((z + s) % NZ) * NX + x, col)

    def in_copy(r):
        return pltpu.make_async_copy(cost_hbm.at[r], cost.at[r], in_sem.at[r])

    def tlm_copy():
        return pltpu.make_async_copy(tlm_hbm.at[pl.ds(me * 8, 8)], tlm, in_sem.at[ROWS])

    def start_in(r, _):
        in_copy(r).start()
        return 0

    lax.fori_loop(0, ROWS, start_in, 0)
    tlm_copy().start()

    barrier = pltpu.get_barrier_semaphore()

    def greet_plane(s, _):
        pl.semaphore_signal(barrier, inc=1, device_id=plane_peer(s)[0], device_id_type=MESH)
        return 0

    def greet_z(s, _):
        pl.semaphore_signal(barrier, inc=1, device_id=z_peer(s), device_id_type=MESH)
        return 0

    lax.fori_loop(1, PLANE, greet_plane, 0)
    lax.fori_loop(1, NZ, greet_z, 0)

    lane = lax.broadcasted_iota(jnp.int32, (BS, 128), 1)
    sub = lax.broadcasted_iota(jnp.int32, (BS, 128), 0)
    sub32 = lax.broadcasted_iota(jnp.int32, (ENT, 128), 0)
    lane32 = lax.broadcasted_iota(jnp.int32, (ENT, 128), 1)
    in_lane = jnp.full((8, 128), -1, jnp.int32)
    in_row = jnp.zeros((ENT, 128), jnp.int32)
    for e in range(ENT):
        c = cand_ref[e % KK, e // KK]
        in_lane = jnp.where(lax.broadcasted_iota(jnp.int32, (8, 128), 1) == e, c, in_lane)
        in_row = jnp.where(sub32 == e, c, in_row)
    lanes32 = jnp.broadcast_to(in_lane[0:1], (ENT, 128))
    equal = jnp.where(in_row == lanes32, 1.0, 0.0)
    same[...] = equal
    earlier = jnp.max(jnp.where(sub32 < lane32, equal, 0.0), axis=0, keepdims=True)
    onehot[...] = jnp.where(
        sub == jnp.broadcast_to(in_lane[0:1], (BS, 128)), 1.0, 0.0
    ) * (1.0 - jnp.broadcast_to(earlier, (BS, 128)))
    missing = jnp.where(jnp.sum(onehot[...], axis=1, keepdims=True) > 0.5, 0.0, LOWEST)

    for step in range(ITERS):
        def source_row(r, _):
            if step == 0:
                in_copy(r).wait()
            mine = lane[:SLAB] == r
            if step > 0:
                shifts, shifts_b = [], []
                for k in range(KK):
                    c = cand_ref[k, r]
                    t = t_recv[step - 1, c // 8, pl.ds(c % 8, 1), :]
                    shifts.append(t)
                    shifts_b.append((t * UNSCALE).astype(jnp.bfloat16))
            for i in range(0, BS, SLAB):
                rows = slice(i, i + SLAB)
                tops = None
                for k in range(KK):
                    for h in (0, 128):
                        v = -cost[r, k, rows, h:h + 128]
                        if step > 0:
                            v = v + shifts_b[k][:, h:h + 128]
                        tops = v if tops is None else jnp.maximum(tops, v)
                top = jnp.max(tops.astype(jnp.float32), axis=1, keepdims=True) * SCALE
                total = None
                for k in range(KK):
                    for h in (0, 128):
                        if step == 0:
                            v = cost[r, k, rows, h:h + 128].astype(jnp.float32) * SCALE
                            c2[r, k, rows, h:h + 128] = v
                            v = -v
                        else:
                            v = shifts[k][:, h:h + 128] - c2[r, k, rows, h:h + 128]
                        p = jnp.exp2(v - top)
                        total = p if total is None else total + p
                total = jnp.sum(total, axis=1, keepdims=True)
                xm[rows, :] = jnp.where(mine, top, xm[rows, :])
                xs[rows, :] = jnp.where(mine, total, xs[rows, :])
            return 0

        lax.fori_loop(0, ROWS, source_row, 0)
        part = xm[...].T[:ROWS] + jnp.log2(xs[...].T[:ROWS])
        a_src[step] = part
        a_recv[step, col] = part
        if step == 0:
            pl.semaphore_wait(barrier, PLANE - 1 + NZ - 1)

        def send_a(s, _):
            pltpu.make_async_remote_copy(
                src_ref=a_src.at[step], dst_ref=a_recv.at[step, col],
                send_sem=a_ss.at[step], recv_sem=a_rs.at[step],
                device_id=plane_peer(s)[0], device_id_type=MESH,
            ).start()
            return 0

        lax.fori_loop(1, NCOL, send_a, 0)
        seven = a_recv.at[step, pl.ds(0, NCOL - 1)]
        pltpu.make_async_copy(seven, seven, a_rs.at[step]).wait()
        source = slm_ref[...] * LOG2E - lse2(a_recv[step])
        if step == ITERS - 1:
            src_out[...] = source * UNSCALE
        st[...] = jnp.concatenate([source, jnp.zeros((128 - ROWS, BS), jnp.float32)], axis=0).T

        def target_row(g, q):
            r = g * GROUP + q
            column = jnp.sum(jnp.where(lane == r, st[...], 0.0), axis=1, keepdims=True)
            wide = jnp.broadcast_to(column, (BS, 128))
            wide_b = (wide * UNSCALE).astype(jnp.bfloat16)
            for k in range(KK):
                for h in (0, 128):
                    v = wide_b - cost[r, k, :, h:h + 128]
                    half = jnp.max(v.reshape(BS // 16, 16, 128), axis=0)
                    top = jnp.max(half.astype(jnp.float32), axis=0, keepdims=True) * SCALE
                    total = None
                    for i in range(0, BS, SLAB):
                        v = (wide[i:i + SLAB] - top) - c2[r, k, i:i + SLAB, h:h + 128]
                        p = jnp.sum(jnp.exp2(v).reshape(SLAB // 8, 8, 128), axis=0)
                        total = p if total is None else total + p
                    total = jnp.sum(total, axis=0, keepdims=True)
                    j = q * KK + k
                    ment[g, j:j + 1, h:h + 128] = top
                    sent[g, j:j + 1, h:h + 128] = total

        def target_rows(g, _):
            for q in range(GROUP):
                target_row(g, q)
            return 0

        lax.fori_loop(0, ROWS // GROUP, target_rows, 0)
        entries = (ment[...] + jnp.log2(sent[...])).reshape(ENT, BS)
        peak = jnp.full((ENT, BS), LOWEST, jnp.float32)
        for e in range(ENT):
            hit = same[:, e:e + 1] > 0.5
            peak = jnp.maximum(peak, jnp.where(hit, entries[e:e + 1], LOWEST))
        mass = jnp.dot(same[:, :ENT], jnp.exp2(entries - peak), precision=HIGHEST,
                       preferred_element_type=jnp.float32)
        merged = peak + jnp.log2(mass)
        spread = jnp.dot(onehot[:, :ENT], merged, precision=HIGHEST,
                         preferred_element_type=jnp.float32) + missing
        dense[step] = spread.reshape(PLANE, 8, BS)
        r_recv[step, me] = dense[step, me]

        def send_r(s, _):
            peer, index = plane_peer(s)
            pltpu.make_async_remote_copy(
                src_ref=dense.at[step, index], dst_ref=r_recv.at[step, me],
                send_sem=r_ss.at[step], recv_sem=r_rs.at[step],
                device_id=peer, device_id_type=MESH,
            ).start()
            return 0

        lax.fori_loop(1, PLANE, send_r, 0)
        others = r_recv.at[step, pl.ds(0, PLANE - 1)]
        pltpu.make_async_copy(others, others, r_rs.at[step]).wait()
        part = lse2(r_recv[step])
        z_src[step] = part
        z_recv[step, z] = part

        def send_z(s, _):
            pltpu.make_async_remote_copy(
                src_ref=z_src.at[step], dst_ref=z_recv.at[step, z],
                send_sem=z_ss.at[step], recv_sem=z_rs.at[step],
                device_id=z_peer(s), device_id_type=MESH,
            ).start()
            return 0

        lax.fori_loop(1, NZ, send_z, 0)
        seven = z_recv.at[step, pl.ds(0, NZ - 1)]
        pltpu.make_async_copy(seven, seven, z_rs.at[step]).wait()
        if step == 0:
            tlm_copy().wait()
        target = tlm[...] * LOG2E - lse2(z_recv[step])
        t_src[step] = target
        t_recv[step, me] = target

        def send_t(s, _):
            pltpu.make_async_remote_copy(
                src_ref=t_src.at[step], dst_ref=t_recv.at[step, me],
                send_sem=t_ss.at[step], recv_sem=t_rs.at[step],
                device_id=plane_peer(s)[0], device_id_type=MESH,
            ).start()
            return 0

        lax.fori_loop(1, PLANE, send_t, 0)
        others = t_recv.at[step, pl.ds(0, PLANE - 1)]
        pltpu.make_async_copy(others, others, t_rs.at[step]).wait()

    tgt_out[...] = t_recv[ITERS - 1]

    for step in range(ITERS):
        for buf, n, sem in (
            (a_recv, NCOL - 1, a_ss), (r_recv, PLANE - 1, r_ss),
            (z_recv, NZ - 1, z_ss), (t_recv, PLANE - 1, t_ss),
        ):
            ref = buf.at[step, pl.ds(0, n)]
            pltpu.make_async_copy(ref, ref, sem.at[step]).wait()


def per_device(block_cost, candidates, source_logmass, target_logmass):
    f32 = jnp.float32
    vmem = pl.BlockSpec(memory_space=pltpu.VMEM)
    dma = pltpu.SemaphoreType.DMA
    source, target = pl.pallas_call(
        body,
        name="sinkhorn",
        out_shape=(
            jax.ShapeDtypeStruct((ROWS, BS), f32),
            jax.ShapeDtypeStruct((PLANE, 8, BS), f32),
        ),
        in_specs=[
            pl.BlockSpec(memory_space=pltpu.SMEM),
            pl.BlockSpec(memory_space=pl.ANY),
            vmem,
            pl.BlockSpec(memory_space=pl.ANY),
        ],
        out_specs=(vmem, vmem),
        scratch_shapes=[
            pltpu.VMEM((ROWS, KK, BS, BS), jnp.bfloat16),
            pltpu.VMEM((ROWS, KK, BS, BS), f32),
            pltpu.VMEM((8, BS), f32),
            pltpu.VMEM((BS, 128), f32),
            pltpu.VMEM((BS, 128), f32),
            pltpu.VMEM((BS, 128), f32),
            pltpu.VMEM((ENT // 8, 8, BS), f32),
            pltpu.VMEM((ENT // 8, 8, BS), f32),
            pltpu.VMEM((BS, 128), f32),
            pltpu.VMEM((ENT, 128), f32),
            pltpu.VMEM((ITERS, ROWS, BS), f32),
            pltpu.VMEM((ITERS, NCOL, ROWS, BS), f32),
            pltpu.VMEM((ITERS, PLANE, 8, BS), f32),
            pltpu.VMEM((ITERS, PLANE, 8, BS), f32),
            pltpu.VMEM((ITERS, 8, BS), f32),
            pltpu.VMEM((ITERS, NZ, 8, BS), f32),
            pltpu.VMEM((ITERS, 8, BS), f32),
            pltpu.VMEM((ITERS, PLANE, 8, BS), f32),
            dma((ROWS + 1,)),
        ] + [dma((ITERS,))] * 8,
        compiler_params=pltpu.CompilerParams(
            collective_id=0, has_side_effects=True, vmem_limit_bytes=60 << 20
        ),
    )(candidates.T, block_cost, source_logmass, target_logmass)
    return source, (target * UNSCALE).reshape(target_logmass.shape)


def solution(mesh):
    return jax.shard_map(
        per_device,
        mesh=mesh,
        in_specs=(P("row", "col", None, None), P("row", "col"), P("row", None), P()),
        out_specs=(P("row", None), P()),
        check_vma=False,
    )
```

```python
import math

import jax
import jax.numpy as jnp
from jax import lax
from jax.experimental import pallas as pl
from jax.experimental.pallas import tpu as pltpu
from jax.sharding import PartitionSpec as P

ITERS = 2
EPS = 0.05
LOG2E = math.log2(math.e)
SCALE = LOG2E / EPS
UNSCALE = EPS / LOG2E
LOWEST = -1e30
MESH = pl.DeviceIdType.MESH
NX, NY, NZ, NC = 4, 4, 8, 2
PLANE = NX * NY * NC
NCOL = NY * NC
ROWS, KK, BS = 16, 2, 256
ENT = ROWS * KK
HALF = 128
CHUNK = 4
CHUNKS = ROWS // CHUNK
SLAB = 64
F32, BF16 = jnp.float32, jnp.bfloat16


def lse2(parts):
    top = jnp.max(parts, axis=0)
    return top + jnp.log2(jnp.sum(jnp.exp2(parts - top[None]), axis=0))


def body(
    cand_ref, cost_hbm, slm_ref, tlm_hbm, src_out, tgt_out,
    cost, c2, cost_t, c2_t, tlm, slm, spot, st, gath, gath_t, m2, s2,
    ment, sent, named, onehot, missing,
    a_src, a_recv, dense, r_recv, z_src, z_recv, t_src, t_recv00, t_recv01, t_recv10, t_recv11,
    in_sem, a_ss, a_rs, r_ss, r_rs, z_ss, z_rs, t_ss, t_rs,
):
    t_recv = ((t_recv00, t_recv01), (t_recv10, t_recv11))
    row, col = lax.axis_index("row"), lax.axis_index("col")
    z, x = row // NX, row % NX
    y, co = col // NC, col % NC
    me = x * NCOL + col

    def plane_peer(s):
        px = (x + s // NCOL) % NX
        pc = ((y + (s // NC) % NY) % NY) * NC + (co + s) % NC
        return (z * NX + px, pc), px * NCOL + pc

    def z_peer(s):
        return (((z + s) % NZ) * NX + x, col)

    def in_copy(r):
        return pltpu.make_async_copy(cost_hbm.at[r], cost.at[r], in_sem.at[r])

    def tlm_copy():
        return pltpu.make_async_copy(tlm_hbm.at[pl.ds(me * 8, 8)], tlm, in_sem.at[ROWS])

    def start_in(r, _):
        in_copy(r).start()
        return 0

    lax.fori_loop(0, ROWS, start_in, 0)
    tlm_copy().start()

    barrier = pltpu.get_barrier_semaphore()

    def greet_plane(s, _):
        pl.semaphore_signal(barrier, inc=1, device_id=plane_peer(s)[0], device_id_type=MESH)
        return 0

    def greet_z(s, _):
        pl.semaphore_signal(barrier, inc=1, device_id=z_peer(s), device_id_type=MESH)
        return 0

    lax.fori_loop(1, PLANE, greet_plane, 0)
    lax.fori_loop(1, NZ, greet_z, 0)

    def landed(buf, n, sem):
        ref = buf.at[pl.ds(0, n)]
        pltpu.make_async_copy(ref, ref, sem).wait()

    for g in range(CHUNKS):
        slm[g] = slm_ref[g * CHUNK:(g + 1) * CHUNK] * LOG2E

    def cand(e):
        return cand_ref[e % KK, e // KK]

    sub32 = lax.broadcasted_iota(jnp.int32, (ENT, HALF), 0)
    lane32 = lax.broadcasted_iota(jnp.int32, (ENT, HALF), 1)
    lane8 = lax.broadcasted_iota(jnp.int32, (8, HALF), 1)
    in_lane = jnp.full((8, HALF), -1, jnp.int32)
    in_row = jnp.zeros((ENT, HALF), jnp.int32)
    for e in range(ENT):
        c = cand(e)
        in_lane = jnp.where(lane8 % ENT == e, c, in_lane)
        in_row = jnp.where(sub32 == e, c, in_row)
    named[...] = in_row
    earlier = jnp.max(
        jnp.where((sub32 < lane32 % ENT) & (in_row == jnp.broadcast_to(in_lane[0:1], (ENT, HALF))), 1.0, 0.0),
        axis=0, keepdims=True)
    in_lane = jnp.where(lane8 < 3 * ENT, in_lane, -1)[0:1]
    sub = lax.broadcasted_iota(jnp.int32, (BS, HALF), 0)
    hot = jnp.where(sub == jnp.broadcast_to(in_lane, (BS, HALF)), 1.0, 0.0)
    hot = hot * (1.0 - jnp.broadcast_to(earlier, (BS, HALF)))
    onehot[...] = hot.astype(BF16)
    absent = jnp.where(jnp.sum(hot, axis=1, keepdims=True) > 0.5, 0.0, LOWEST)
    missing[...] = jnp.broadcast_to(absent, (BS, HALF))

    lane = lax.broadcasted_iota(jnp.int32, (SLAB, HALF), 1)

    def send_chunk(step, g, part):
        a_src[step, g] = part
        a_recv[step, g, col] = part

        def send(s, _):
            pltpu.make_async_remote_copy(
                src_ref=a_src.at[step, g], dst_ref=a_recv.at[step, g, col],
                send_sem=a_ss.at[step], recv_sem=a_rs.at[step, g],
                device_id=plane_peer(s)[0], device_id_type=MESH,
            ).start()
            return 0

        lax.fori_loop(1, NCOL, send, 0)

    def first_chunk(g):
        for q in range(CHUNK):
            in_copy(g * CHUNK + q).wait()
        packed = []
        for i in range(0, BS, SLAB):
            rows = slice(i, i + SLAB)
            keep = jnp.zeros((SLAB, HALF), F32)
            for q in range(CHUNK):
                r = g * CHUNK + q
                parts = [cost[r, k, rows, h:h + HALF] for k in range(KK) for h in (0, HALF)]
                low = jnp.minimum(jnp.minimum(parts[0], parts[1]), jnp.minimum(parts[2], parts[3]))
                low = jnp.min(low.astype(F32), axis=1, keepdims=True) * SCALE
                total = None
                for p in parts:
                    p = jnp.exp2(low - p.astype(F32) * SCALE)
                    total = p if total is None else total + p
                total = jnp.sum(total, axis=1, keepdims=True)
                keep = jnp.where(lane == q, low, keep)
                keep = jnp.where(lane == CHUNK + q, total, keep)
            packed.append(keep)
        flat = jnp.concatenate(packed, axis=0).T
        return jnp.log2(flat[CHUNK:2 * CHUNK]) - flat[:CHUNK]

    send_chunk(0, 0, first_chunk_after_barrier(first_chunk, barrier))

    def first_rest(g, _):
        send_chunk(0, g, first_chunk(g))
        return 0

    lax.fori_loop(1, CHUNKS, first_rest, 0)

    def scale_costs(r, _):
        for k in range(KK):
            for i in range(0, BS, SLAB):
                c2[r, k, i:i + SLAB] = cost[r, k, i:i + SLAB].astype(F32) * SCALE
        return 0

    lax.fori_loop(0, ROWS, scale_costs, 0)

    def transpose_costs(r, _):
        for k in range(KK):
            turned = cost[r, k].T
            cost_t[r, k] = turned
            c2_t[r, k] = turned.astype(F32) * SCALE
        return 0

    def gather(step, h):
        for e in range(ENT):
            c = cand(e)
            gath[e // 8, e % 8:e % 8 + 1, :] = t_recv[step - 1][h][c // 8, pl.ds(c % 8, 1), :]
        for g in range(CHUNKS):
            gath_t[h, g] = gath[g].T

    def source_half(g, h):
        js = slice(h * HALF, (h + 1) * HALF)
        for q in range(CHUNK):
            r = g * CHUNK + q
            wide = [jnp.broadcast_to(gath_t[h, g, :, q * KK + k:q * KK + k + 1], (HALF, HALF)) for k in range(KK)]
            wide_b = [(w * UNSCALE).astype(BF16) for w in wide]
            for i in (0, HALF):
                top = None
                for k in range(KK):
                    v = wide_b[k] - cost_t[r, k, js, i:i + HALF]
                    v = jnp.max(v.reshape(HALF // 16, 16, HALF), axis=0)
                    top = v if top is None else jnp.maximum(top, v)
                top = jnp.max(top.astype(F32), axis=0, keepdims=True) * SCALE
                total = None
                for k in range(KK):
                    for j in range(0, HALF, SLAB):
                        v = (wide[k][j:j + SLAB] - top) - c2_t[r, k, h * HALF + j:h * HALF + j + SLAB, i:i + HALF]
                        p = jnp.sum(jnp.exp2(v).reshape(SLAB // 8, 8, HALF), axis=0)
                        total = p if total is None else total + p
                m2[h, g, q:q + 1, i:i + HALF] = top
                s2[h, g, q:q + 1, i:i + HALF] = jnp.sum(total, axis=0, keepdims=True)

    def both_halves(g):
        top = jnp.maximum(m2[0, g], m2[1, g])
        total = s2[0, g] * jnp.exp2(m2[0, g] - top) + s2[1, g] * jnp.exp2(m2[1, g] - top)
        return top + jnp.log2(total)

    def take_chunk(step, g):
        landed(a_recv.at[step, g], NCOL - 1, a_rs.at[step, g])
        source = slm[g] - lse2(a_recv[step, g])
        if step == ITERS - 1:
            spot[g] = source * UNSCALE
        st[g] = jnp.concatenate([source, jnp.zeros_like(source)], axis=0).T

    def target_part(g, halves):
        for q in range(CHUNK):
            r = g * CHUNK + q
            wide = jnp.broadcast_to(st[g, :, q:q + 1], (BS, HALF))
            wide_b = (wide * UNSCALE).astype(BF16)
            for k in range(KK):
                for h in halves:
                    js = slice(h * HALF, (h + 1) * HALF)
                    v = wide_b - cost[r, k, :, js]
                    v = jnp.max(v.reshape(BS // 16, 16, HALF), axis=0)
                    top = jnp.max(v.astype(F32), axis=0, keepdims=True) * SCALE
                    total = None
                    for i in range(0, BS, SLAB):
                        v = (wide[i:i + SLAB] - top) - c2[r, k, i:i + SLAB, js]
                        p = jnp.sum(jnp.exp2(v).reshape(SLAB // 8, 8, HALF), axis=0)
                        total = p if total is None else total + p
                    j = q * KK + k
                    ment[h, g, j:j + 1, :] = top
                    sent[h, g, j:j + 1, :] = jnp.sum(total, axis=0, keepdims=True)

    def scatter(step, h):
        entries = (ment[h] + jnp.log2(sent[h])).reshape(ENT, HALF)
        blocks = named[...]
        peak = jnp.full((ENT, HALF), LOWEST, F32)
        for e in range(ENT):
            peak = jnp.maximum(peak, jnp.where(blocks == cand(e), entries[e:e + 1], LOWEST))
        shares = jnp.exp2(entries - peak)
        mass = jnp.zeros((ENT, HALF), F32)
        for e in range(ENT):
            mass = mass + jnp.where(blocks == cand(e), shares[e:e + 1], 0.0)
        merged = peak + jnp.log2(mass)
        first = merged.astype(BF16)
        rest = merged - first.astype(F32)
        second = rest.astype(BF16)
        third = (rest - second.astype(F32)).astype(BF16)
        pieces = jnp.concatenate([first, second, third, jnp.zeros_like(third)], axis=0)
        spread = jnp.dot(onehot[...], pieces, preferred_element_type=F32) + missing[...]
        dense[step, h] = spread.reshape(PLANE, 8, HALF)
        r_recv[step, h, me] = dense[step, h, me]

        def send(s, _):
            peer, index = plane_peer(s)
            pltpu.make_async_remote_copy(
                src_ref=dense.at[step, h, index], dst_ref=r_recv.at[step, h, me],
                send_sem=r_ss.at[step, h], recv_sem=r_rs.at[step, h],
                device_id=peer, device_id_type=MESH,
            ).start()
            return 0

        lax.fori_loop(1, PLANE, send, 0)

    def along_z(step, h):
        landed(r_recv.at[step, h], PLANE - 1, r_rs.at[step, h])
        part = lse2(r_recv[step, h])
        z_src[step, h] = part
        z_recv[step, h, z] = part

        def send(s, _):
            pltpu.make_async_remote_copy(
                src_ref=z_src.at[step, h], dst_ref=z_recv.at[step, h, z],
                send_sem=z_ss.at[step, h], recv_sem=z_rs.at[step, h],
                device_id=z_peer(s), device_id_type=MESH,
            ).start()
            return 0

        lax.fori_loop(1, NZ, send, 0)

    def spread_target(step, h):
        landed(z_recv.at[step, h], NZ - 1, z_rs.at[step, h])
        target = tlm[:, h * HALF:(h + 1) * HALF] * LOG2E - lse2(z_recv[step, h])
        t_src[step, h] = target
        t_recv[step][h][me] = target

        def send(s, _):
            pltpu.make_async_remote_copy(
                src_ref=t_src.at[step, h], dst_ref=t_recv[step][h].at[me],
                send_sem=t_ss.at[step, h], recv_sem=t_rs.at[step, h],
                device_id=plane_peer(s)[0], device_id_type=MESH,
            ).start()
            return 0

        lax.fori_loop(1, PLANE, send, 0)

    for step in range(ITERS):
        if step > 0:
            for h in range(2):
                landed(t_recv[step - 1][h], PLANE - 1, t_rs.at[step - 1, h])
                gather(step, h)

                def source_rows(g, _):
                    source_half(g, h)
                    if h == 1:
                        send_chunk(step, g, both_halves(g))
                    return 0

                lax.fori_loop(0, CHUNKS, source_rows, 0)

        def target_rows(g, _):
            take_chunk(step, g)
            target_part(g, (0, 1))
            return 0

        lax.fori_loop(0, CHUNKS - 1, target_rows, 0)
        take_chunk(step, CHUNKS - 1)
        target_part(CHUNKS - 1, (0,))
        scatter(step, 0)
        target_part(CHUNKS - 1, (1,))
        scatter(step, 1)
        if step == 0:
            tlm_copy().wait()
            lax.fori_loop(0, ROWS // 2, transpose_costs, 0)
        along_z(step, 0)
        along_z(step, 1)
        if step == 0:
            lax.fori_loop(ROWS // 2, ROWS, transpose_costs, 0)
        spread_target(step, 0)
        spread_target(step, 1)

    for g in range(CHUNKS):
        src_out[g * CHUNK:(g + 1) * CHUNK] = spot[g]
    for h in range(2):
        landed(t_recv[ITERS - 1][h], PLANE - 1, t_rs.at[ITERS - 1, h])
        tgt_out[:, h * HALF:(h + 1) * HALF] = t_recv[ITERS - 1][h][...].reshape(PLANE * 8, HALF) * UNSCALE

    for step in range(ITERS):
        ref = a_recv.at[step, :, pl.ds(0, NCOL - 1)]
        pltpu.make_async_copy(ref, ref, a_ss.at[step]).wait()
        for h in range(2):
            landed(r_recv.at[step, h], PLANE - 1, r_ss.at[step, h])
            landed(z_recv.at[step, h], NZ - 1, z_ss.at[step, h])
            landed(t_recv[step][h], PLANE - 1, t_ss.at[step, h])


def first_chunk_after_barrier(first_chunk, barrier):
    part = first_chunk(0)
    pl.semaphore_wait(barrier, PLANE - 1 + NZ - 1)
    return part


def per_device(block_cost, candidates, source_logmass, target_logmass):
    vmem = pl.BlockSpec(memory_space=pltpu.VMEM)
    hbm = pl.BlockSpec(memory_space=pl.ANY)
    dma = pltpu.SemaphoreType.DMA
    scratch = [
        ((ROWS, KK, BS, BS), BF16),
        ((ROWS, KK, BS, BS), F32),
        ((ROWS, KK, BS, BS), BF16),
        ((ROWS, KK, BS, BS), F32),
        ((8, BS), F32),
        ((CHUNKS, CHUNK, BS), F32),
        ((CHUNKS, CHUNK, BS), F32),
        ((CHUNKS, BS, 8), F32),
        ((ENT // 8, 8, HALF), F32),
        ((2, CHUNKS, HALF, 8), F32),
        ((2, CHUNKS, CHUNK, BS), F32),
        ((2, CHUNKS, CHUNK, BS), F32),
        ((2, ENT // 8, 8, HALF), F32),
        ((2, ENT // 8, 8, HALF), F32),
        ((ENT, HALF), jnp.int32),
        ((BS, HALF), BF16),
        ((BS, HALF), F32),
        ((ITERS, CHUNKS, CHUNK, BS), F32),
        ((ITERS, CHUNKS, NCOL, CHUNK, BS), F32),
        ((ITERS, 2, PLANE, 8, HALF), F32),
        ((ITERS, 2, PLANE, 8, HALF), F32),
        ((ITERS, 2, 8, HALF), F32),
        ((ITERS, 2, NZ, 8, HALF), F32),
        ((ITERS, 2, 8, HALF), F32),
    ] + [((PLANE, 8, HALF), F32)] * (2 * ITERS)
    return pl.pallas_call(
        body,
        name="sinkhorn",
        out_shape=(
            jax.ShapeDtypeStruct(source_logmass.shape, F32),
            jax.ShapeDtypeStruct(target_logmass.shape, F32),
        ),
        in_specs=[pl.BlockSpec(memory_space=pltpu.SMEM), hbm, vmem, hbm],
        out_specs=(vmem, vmem),
        scratch_shapes=[pltpu.VMEM(*s) for s in scratch]
        + [dma((ROWS + 1,)), dma((ITERS,)), dma((ITERS, CHUNKS))]
        + [dma((ITERS, 2))] * 6,
        compiler_params=pltpu.CompilerParams(
            collective_id=0, has_side_effects=True, vmem_limit_bytes=60 << 20
        ),
    )(candidates.T, block_cost, source_logmass, target_logmass)


def solution(mesh):
    return jax.shard_map(
        per_device,
        mesh=mesh,
        in_specs=(P("row", "col", None, None), P("row", "col"), P("row", None), P()),
        out_specs=(P("row", None), P()),
        check_vma=False,
    )
```

```python
import math

import jax
import jax.numpy as jnp
from jax import lax
from jax.experimental import pallas as pl
from jax.experimental.pallas import tpu as pltpu
from jax.sharding import PartitionSpec as P

ITERS = 2
EPS = 0.05
LOG2E = math.log2(math.e)
SCALE = LOG2E / EPS
UNSCALE = EPS / LOG2E
LOWEST = -1e30
MESH = pl.DeviceIdType.MESH
NX, NY, NZ, NC = 4, 4, 8, 2
PLANE = NX * NY * NC
NCOL = NY * NC
ROWS, KK, BS = 16, 2, 256
ENT = ROWS * KK
HALF = 128
CHUNK = 4
CHUNKS = ROWS // CHUNK
SLAB = 64
F32, BF16 = jnp.float32, jnp.bfloat16


def lse2(parts):
    top = jnp.max(parts, axis=0)
    return top + jnp.log2(jnp.sum(jnp.exp2(parts - top[None]), axis=0))


def body(
    cand_ref, cost_hbm, slm_ref, tlm_hbm, src_out, tgt_out,
    cost, c2, cost_t, c2_t, tlm, slm, spot, st, gath, gath_t, m2, s2,
    ment, sent, named, onehot, missing,
    a_src, a_recv, dense, r_recv, z_src, z_recv, t_src, t_recv00, t_recv01, t_recv10, t_recv11,
    in_sem, a_ss, a_rs, r_ss, r_rs, z_ss, z_rs, t_ss, t_rs,
):
    t_recv = ((t_recv00, t_recv01), (t_recv10, t_recv11))
    row, col = lax.axis_index("row"), lax.axis_index("col")
    z, x = row // NX, row % NX
    y, co = col // NC, col % NC
    me = x * NCOL + col

    def wrap(v, n):
        return jnp.where(v >= n, v - n, v)

    xs = [wrap(x + d, NX) for d in range(NX)]
    ys = [wrap(y + d, NY) for d in range(NY)]
    cs = [co, 1 - co]
    zrows = [wrap(z + d, NZ) * NX + x for d in range(NZ)]
    xrows = [z * NX + v for v in xs]
    cols = [v * NC + c for v in ys for c in cs]

    def hops(s):
        return min(s // NCOL, NX - s // NCOL) + min(s % NCOL // NC, NY - s % NCOL // NC)

    FAR_PLANE = sorted(range(1, PLANE), key=lambda s: -hops(s))
    FAR_COL = sorted(range(1, NCOL), key=lambda s: -hops(s))
    FAR_Z = sorted(range(1, NZ), key=lambda s: -min(s, NZ - s))

    def plane_peer(s):
        return (xrows[s // NCOL], cols[s % NCOL]), xs[s // NCOL] * NCOL + cols[s % NCOL]

    def z_peer(s):
        return (zrows[s], col)

    def in_copy(r):
        return pltpu.make_async_copy(cost_hbm.at[r], cost.at[r], in_sem.at[r])

    def tlm_copy():
        return pltpu.make_async_copy(tlm_hbm.at[pl.ds(me * 8, 8)], tlm, in_sem.at[ROWS])

    for r in range(ROWS):
        in_copy(r).start()
    barrier = pltpu.get_barrier_semaphore()
    for s in FAR_Z:
        pl.semaphore_signal(barrier, inc=1, device_id=z_peer(s), device_id_type=MESH)
    for s in FAR_PLANE:
        pl.semaphore_signal(barrier, inc=1, device_id=plane_peer(s)[0], device_id_type=MESH)
    tlm_copy().start()

    def landed(buf, n, sem):
        ref = buf.at[pl.ds(0, n)]
        pltpu.make_async_copy(ref, ref, sem).wait()

    def cand(e):
        return cand_ref[e % KK, e // KK]

    def tables():
        for g in range(CHUNKS):
            slm[g] = slm_ref[g * CHUNK:(g + 1) * CHUNK] * LOG2E

        sub32 = lax.broadcasted_iota(jnp.int32, (ENT, HALF), 0)
        lane32 = lax.broadcasted_iota(jnp.int32, (ENT, HALF), 1)
        lane8 = lax.broadcasted_iota(jnp.int32, (8, HALF), 1)
        in_lane = jnp.full((8, HALF), -1, jnp.int32)
        in_row = jnp.zeros((ENT, HALF), jnp.int32)
        for e in range(ENT):
            c = cand(e)
            in_lane = jnp.where(lane8 % ENT == e, c, in_lane)
            in_row = jnp.where(sub32 == e, c, in_row)
        named[...] = in_row
        earlier = jnp.max(
            jnp.where((sub32 < lane32 % ENT) & (in_row == jnp.broadcast_to(in_lane[0:1], (ENT, HALF))), 1.0, 0.0),
            axis=0, keepdims=True)
        in_lane = jnp.where(lane8 < 3 * ENT, in_lane, -1)[0:1]
        sub = lax.broadcasted_iota(jnp.int32, (BS, HALF), 0)
        hot = jnp.where(sub == jnp.broadcast_to(in_lane, (BS, HALF)), 1.0, 0.0)
        hot = hot * (1.0 - jnp.broadcast_to(earlier, (BS, HALF)))
        onehot[...] = hot.astype(BF16)
        absent = jnp.where(jnp.sum(hot, axis=1, keepdims=True) > 0.5, 0.0, LOWEST)
        missing[...] = jnp.broadcast_to(absent, (BS, HALF))

    def keep_chunk(step, g, part):
        a_src[step, g] = part
        a_recv[step, g, col] = part

    def send_chunk(step, g):
        for s in FAR_COL:
            pltpu.make_async_remote_copy(
                src_ref=a_src.at[step, g], dst_ref=a_recv.at[step, g, col],
                send_sem=a_ss.at[step], recv_sem=a_rs.at[step, g],
                device_id=plane_peer(s)[0], device_id_type=MESH,
            ).start()

    def first_chunk(g, _):
        found = []
        for q in range(CHUNK):
            in_copy(g * CHUNK + q).wait()
        for q in range(CHUNK):
            r = g * CHUNK + q
            turned = [cost[r, k].T for k in range(KK)]
            for k in range(KK):
                cost_t[r, k] = turned[k]
            halves = []
            for i in (0, HALF):
                low = None
                for k in range(KK):
                    v = jnp.min(turned[k][:, i:i + HALF].reshape(BS // 16, 16, HALF), axis=0)
                    low = v if low is None else jnp.minimum(low, v)
                low = jnp.min(low.astype(F32), axis=0, keepdims=True) * SCALE
                total = None
                for k in range(KK):
                    p = jnp.exp2(low - turned[k][:, i:i + HALF].astype(F32) * SCALE)
                    p = jnp.sum(p.reshape(BS // 8, 8, HALF), axis=0)
                    total = p if total is None else total + p
                halves.append(jnp.log2(jnp.sum(total, axis=0, keepdims=True)) - low)
            found.append(jnp.concatenate(halves, axis=1))
        keep_chunk(0, g, jnp.concatenate(found, axis=0))
        return 0

    lax.fori_loop(0, CHUNKS, first_chunk, 0)
    pl.semaphore_wait(barrier, PLANE - 1 + NZ - 1)
    for g in range(CHUNKS):
        send_chunk(0, g)

    def scale_costs(r, _):
        for k in range(KK):
            for i in range(0, BS, SLAB):
                c2[r, k, i:i + SLAB] = cost[r, k, i:i + SLAB].astype(F32) * SCALE
        return 0

    lax.fori_loop(0, ROWS, scale_costs, 0)
    tables()

    def scale_turned(r, _):
        for k in range(KK):
            for i in range(0, BS, SLAB):
                c2_t[r, k, i:i + SLAB] = cost_t[r, k, i:i + SLAB].astype(F32) * SCALE
        return 0

    def gather(step, h):
        for e in range(ENT):
            c = cand(e)
            gath[e // 8, e % 8:e % 8 + 1, :] = t_recv[step - 1][h][c // 8, pl.ds(c % 8, 1), :]
        for g in range(CHUNKS):
            gath_t[h, g] = gath[g].T

    def source_half(g, h):
        js = slice(h * HALF, (h + 1) * HALF)
        for q in range(CHUNK):
            r = g * CHUNK + q
            wide = [jnp.broadcast_to(gath_t[h, g, :, q * KK + k:q * KK + k + 1], (HALF, HALF)) for k in range(KK)]
            wide_b = [(w * UNSCALE).astype(BF16) for w in wide]
            for i in (0, HALF):
                top = None
                for k in range(KK):
                    v = wide_b[k] - cost_t[r, k, js, i:i + HALF]
                    v = jnp.max(v.reshape(HALF // 16, 16, HALF), axis=0)
                    top = v if top is None else jnp.maximum(top, v)
                top = jnp.max(top.astype(F32), axis=0, keepdims=True) * SCALE
                total = None
                for k in range(KK):
                    for j in range(0, HALF, SLAB):
                        v = (wide[k][j:j + SLAB] - top) - c2_t[r, k, h * HALF + j:h * HALF + j + SLAB, i:i + HALF]
                        p = jnp.sum(jnp.exp2(v).reshape(SLAB // 8, 8, HALF), axis=0)
                        total = p if total is None else total + p
                m2[h, g, q:q + 1, i:i + HALF] = top
                s2[h, g, q:q + 1, i:i + HALF] = jnp.sum(total, axis=0, keepdims=True)

    def both_halves(g):
        top = jnp.maximum(m2[0, g], m2[1, g])
        total = s2[0, g] * jnp.exp2(m2[0, g] - top) + s2[1, g] * jnp.exp2(m2[1, g] - top)
        return top + jnp.log2(total)

    def take_chunk(step, g):
        landed(a_recv.at[step, g], NCOL - 1, a_rs.at[step, g])
        source = slm[g] - lse2(a_recv[step, g])
        if step == ITERS - 1:
            spot[g] = source * UNSCALE
        st[g] = jnp.concatenate([source, jnp.zeros_like(source)], axis=0).T

    def target_part(g, halves):
        for q in range(CHUNK):
            r = g * CHUNK + q
            wide = jnp.broadcast_to(st[g, :, q:q + 1], (BS, HALF))
            wide_b = (wide * UNSCALE).astype(BF16)
            for k in range(KK):
                for h in halves:
                    js = slice(h * HALF, (h + 1) * HALF)
                    v = wide_b - cost[r, k, :, js]
                    v = jnp.max(v.reshape(BS // 16, 16, HALF), axis=0)
                    top = jnp.max(v.astype(F32), axis=0, keepdims=True) * SCALE
                    total = None
                    for i in range(0, BS, SLAB):
                        v = (wide[i:i + SLAB] - top) - c2[r, k, i:i + SLAB, js]
                        p = jnp.sum(jnp.exp2(v).reshape(SLAB // 8, 8, HALF), axis=0)
                        total = p if total is None else total + p
                    j = q * KK + k
                    ment[h, g, j:j + 1, :] = top
                    sent[h, g, j:j + 1, :] = jnp.sum(total, axis=0, keepdims=True)

    def scatter(step, h):
        entries = (ment[h] + jnp.log2(sent[h])).reshape(ENT, HALF)
        blocks = named[...]
        peak = jnp.full((ENT, HALF), LOWEST, F32)
        for e in range(ENT):
            peak = jnp.maximum(peak, jnp.where(blocks == cand(e), entries[e:e + 1], LOWEST))
        shares = jnp.exp2(entries - peak)
        mass = jnp.zeros((ENT, HALF), F32)
        for e in range(ENT):
            mass = mass + jnp.where(blocks == cand(e), shares[e:e + 1], 0.0)
        merged = peak + jnp.log2(mass)
        first = merged.astype(BF16)
        rest = merged - first.astype(F32)
        second = rest.astype(BF16)
        third = (rest - second.astype(F32)).astype(BF16)
        pieces = jnp.concatenate([first, second, third, jnp.zeros_like(third)], axis=0)
        spread = jnp.dot(onehot[...], pieces, preferred_element_type=F32) + missing[...]
        dense[step, h] = spread.reshape(PLANE, 8, HALF)
        r_recv[step, h, me] = dense[step, h, me]

        for s in FAR_PLANE:
            peer, index = plane_peer(s)
            pltpu.make_async_remote_copy(
                src_ref=dense.at[step, h, index], dst_ref=r_recv.at[step, h, me],
                send_sem=r_ss.at[step, h], recv_sem=r_rs.at[step, h],
                device_id=peer, device_id_type=MESH,
            ).start()

    def along_z(step, h):
        landed(r_recv.at[step, h], PLANE - 1, r_rs.at[step, h])
        part = lse2(r_recv[step, h])
        z_src[step, h] = part
        z_recv[step, h, z] = part

        for s in FAR_Z:
            pltpu.make_async_remote_copy(
                src_ref=z_src.at[step, h], dst_ref=z_recv.at[step, h, z],
                send_sem=z_ss.at[step, h], recv_sem=z_rs.at[step, h],
                device_id=z_peer(s), device_id_type=MESH,
            ).start()

    def spread_target(step, h):
        landed(z_recv.at[step, h], NZ - 1, z_rs.at[step, h])
        target = tlm[:, h * HALF:(h + 1) * HALF] * LOG2E - lse2(z_recv[step, h])
        t_src[step, h] = target
        t_recv[step][h][me] = target

        for s in FAR_PLANE:
            pltpu.make_async_remote_copy(
                src_ref=t_src.at[step, h], dst_ref=t_recv[step][h].at[me],
                send_sem=t_ss.at[step, h], recv_sem=t_rs.at[step, h],
                device_id=plane_peer(s)[0], device_id_type=MESH,
            ).start()

    for step in range(ITERS):
        if step > 0:
            for h in range(2):
                landed(t_recv[step - 1][h], PLANE - 1, t_rs.at[step - 1, h])
                gather(step, h)

                def source_rows(g, _):
                    source_half(g, h)
                    if h == 1:
                        keep_chunk(step, g, both_halves(g))
                        send_chunk(step, g)
                    return 0

                lax.fori_loop(0, CHUNKS, source_rows, 0)

        def target_rows(g, _):
            take_chunk(step, g)
            target_part(g, (0, 1))
            return 0

        lax.fori_loop(0, CHUNKS - 1, target_rows, 0)
        take_chunk(step, CHUNKS - 1)
        target_part(CHUNKS - 1, (0,))
        scatter(step, 0)
        target_part(CHUNKS - 1, (1,))
        scatter(step, 1)
        if step == 0:
            tlm_copy().wait()
            lax.fori_loop(0, ROWS, scale_turned, 0)
        along_z(step, 0)
        along_z(step, 1)
        spread_target(step, 0)
        spread_target(step, 1)

    for g in range(CHUNKS):
        src_out[g * CHUNK:(g + 1) * CHUNK] = spot[g]
    for h in range(2):
        landed(t_recv[ITERS - 1][h], PLANE - 1, t_rs.at[ITERS - 1, h])
        tgt_out[:, h * HALF:(h + 1) * HALF] = t_recv[ITERS - 1][h][...].reshape(PLANE * 8, HALF) * UNSCALE

    for step in range(ITERS):
        ref = a_recv.at[step, :, pl.ds(0, NCOL - 1)]
        pltpu.make_async_copy(ref, ref, a_ss.at[step]).wait()
        for h in range(2):
            landed(r_recv.at[step, h], PLANE - 1, r_ss.at[step, h])
            landed(z_recv.at[step, h], NZ - 1, z_ss.at[step, h])
            landed(t_recv[step][h], PLANE - 1, t_ss.at[step, h])


def per_device(block_cost, candidates, source_logmass, target_logmass):
    vmem = pl.BlockSpec(memory_space=pltpu.VMEM)
    hbm = pl.BlockSpec(memory_space=pl.ANY)
    dma = pltpu.SemaphoreType.DMA
    scratch = [
        ((ROWS, KK, BS, BS), BF16),
        ((ROWS, KK, BS, BS), F32),
        ((ROWS, KK, BS, BS), BF16),
        ((ROWS, KK, BS, BS), F32),
        ((8, BS), F32),
        ((CHUNKS, CHUNK, BS), F32),
        ((CHUNKS, CHUNK, BS), F32),
        ((CHUNKS, BS, 8), F32),
        ((ENT // 8, 8, HALF), F32),
        ((2, CHUNKS, HALF, 8), F32),
        ((2, CHUNKS, CHUNK, BS), F32),
        ((2, CHUNKS, CHUNK, BS), F32),
        ((2, ENT // 8, 8, HALF), F32),
        ((2, ENT // 8, 8, HALF), F32),
        ((ENT, HALF), jnp.int32),
        ((BS, HALF), BF16),
        ((BS, HALF), F32),
        ((ITERS, CHUNKS, CHUNK, BS), F32),
        ((ITERS, CHUNKS, NCOL, CHUNK, BS), F32),
        ((ITERS, 2, PLANE, 8, HALF), F32),
        ((ITERS, 2, PLANE, 8, HALF), F32),
        ((ITERS, 2, 8, HALF), F32),
        ((ITERS, 2, NZ, 8, HALF), F32),
        ((ITERS, 2, 8, HALF), F32),
    ] + [((PLANE, 8, HALF), F32)] * (2 * ITERS)
    return pl.pallas_call(
        body,
        name="sinkhorn",
        out_shape=(
            jax.ShapeDtypeStruct(source_logmass.shape, F32),
            jax.ShapeDtypeStruct(target_logmass.shape, F32),
        ),
        in_specs=[pl.BlockSpec(memory_space=pltpu.SMEM), hbm, vmem, hbm],
        out_specs=(vmem, vmem),
        scratch_shapes=[pltpu.VMEM(*s) for s in scratch]
        + [dma((ROWS + 1,)), dma((ITERS,)), dma((ITERS, CHUNKS))]
        + [dma((ITERS, 2))] * 6,
        compiler_params=pltpu.CompilerParams(
            collective_id=0, has_side_effects=True, vmem_limit_bytes=60 << 20
        ),
    )(candidates.T, block_cost, source_logmass, target_logmass)


def solution(mesh):
    return jax.shard_map(
        per_device,
        mesh=mesh,
        in_specs=(P("row", "col", None, None), P("row", "col"), P("row", None), P()),
        out_specs=(P("row", None), P()),
        check_vma=False,
    )
```

```python
import math

import jax
import jax.numpy as jnp
from jax import lax
from jax.experimental import pallas as pl
from jax.experimental.pallas import tpu as pltpu
from jax.sharding import PartitionSpec as P

ITERS = 2
EPS = 0.05
LOG2E = math.log2(math.e)
SCALE = LOG2E / EPS
UNSCALE = EPS / LOG2E
LOWEST = -1e30
MESH = pl.DeviceIdType.MESH
NX, NY, NZ, NC = 4, 4, 8, 2
PLANE = NX * NY * NC
NCOL = NY * NC
ROWS, KK, BS = 16, 2, 256
ENT = ROWS * KK
HALF = 128
CHUNK = 4
CHUNKS = ROWS // CHUNK
SLAB = 64
PIECES = 4
F32, BF16 = jnp.float32, jnp.bfloat16


def lse2(parts):
    top = jnp.max(parts, axis=0)
    return top + jnp.log2(jnp.sum(jnp.exp2(parts - top[None]), axis=0))


def body(
    cand_ref, cost_hbm, slm_ref, tlm_hbm, src_out, tgt_out,
    cost, c2, cost_t, c2_t, tlm, slm, spot, st, gath, gath_t, m2, s2,
    ment, sent, named, onehot, missing,
    a_src, a_recv, dense, r_recv, z_src, z_recv, t_src, t_recv00, t_recv01, t_recv10, t_recv11,
    in_sem, a_ss, a_rs, r_ss, r_rs, z_ss, z_rs, t_ss, t_rs,
):
    t_recv = ((t_recv00, t_recv01), (t_recv10, t_recv11))
    row, col = lax.axis_index("row"), lax.axis_index("col")
    z, x = row // NX, row % NX
    y, co = col // NC, col % NC
    me = x * NCOL + col

    def wrap(v, n):
        return jnp.where(v >= n, v - n, v)

    xs = [wrap(x + d, NX) for d in range(NX)]
    ys = [wrap(y + d, NY) for d in range(NY)]
    cs = [co, 1 - co]
    zrows = [wrap(z + d, NZ) * NX + x for d in range(NZ)]
    xrows = [z * NX + v for v in xs]
    cols = [v * NC + c for v in ys for c in cs]

    def hops(s):
        return min(s // NCOL, NX - s // NCOL) + min(s % NCOL // NC, NY - s % NCOL // NC)

    FAR_PLANE = sorted(range(1, PLANE), key=lambda s: -hops(s))
    FAR_COL = sorted(range(1, NCOL), key=lambda s: -hops(s))
    FAR_Z = sorted(range(1, NZ), key=lambda s: -min(s, NZ - s))

    def plane_peer(s):
        return (xrows[s // NCOL], cols[s % NCOL]), xs[s // NCOL] * NCOL + cols[s % NCOL]

    def z_peer(s):
        return (zrows[s], col)

    def in_copy(r):
        return pltpu.make_async_copy(cost_hbm.at[r], cost.at[r], in_sem.at[r])

    def tlm_copy():
        return pltpu.make_async_copy(tlm_hbm.at[pl.ds(me * 8, 8)], tlm, in_sem.at[ROWS])

    for r in range(ROWS):
        in_copy(r).start()
    barrier = pltpu.get_barrier_semaphore()
    for s in FAR_Z:
        pl.semaphore_signal(barrier, inc=1, device_id=z_peer(s), device_id_type=MESH)
    for s in FAR_PLANE:
        pl.semaphore_signal(barrier, inc=1, device_id=plane_peer(s)[0], device_id_type=MESH)
    tlm_copy().start()

    def landed(buf, n, sem):
        ref = buf.at[pl.ds(0, n)]
        pltpu.make_async_copy(ref, ref, sem).wait()

    def cand(e):
        return cand_ref[e % KK, e // KK]

    def tables():
        for g in range(CHUNKS):
            slm[g] = slm_ref[g * CHUNK:(g + 1) * CHUNK] * LOG2E

        sub32 = lax.broadcasted_iota(jnp.int32, (ENT, HALF), 0)
        lane32 = lax.broadcasted_iota(jnp.int32, (ENT, HALF), 1)
        lane8 = lax.broadcasted_iota(jnp.int32, (8, HALF), 1)
        in_lane = jnp.full((8, HALF), -1, jnp.int32)
        in_row = jnp.zeros((ENT, HALF), jnp.int32)
        for e in range(ENT):
            c = cand(e)
            in_lane = jnp.where(lane8 % ENT == e, c, in_lane)
            in_row = jnp.where(sub32 == e, c, in_row)
        named[...] = in_row
        earlier = jnp.max(
            jnp.where((sub32 < lane32 % ENT) & (in_row == jnp.broadcast_to(in_lane[0:1], (ENT, HALF))), 1.0, 0.0),
            axis=0, keepdims=True)
        in_lane = jnp.where(lane8 < 3 * ENT, in_lane, -1)[0:1]
        sub = lax.broadcasted_iota(jnp.int32, (BS, HALF), 0)
        hot = jnp.where(sub == jnp.broadcast_to(in_lane, (BS, HALF)), 1.0, 0.0)
        hot = hot * (1.0 - jnp.broadcast_to(earlier, (BS, HALF)))
        onehot[...] = hot.astype(BF16)
        absent = jnp.where(jnp.sum(hot, axis=1, keepdims=True) > 0.5, 0.0, LOWEST)
        missing[...] = jnp.broadcast_to(absent, (BS, HALF))

    def keep_chunk(step, g, part):
        a_src[step, g] = part
        a_recv[step, g, col] = part

    def send_chunk(step, g):
        for s in FAR_COL:
            pltpu.make_async_remote_copy(
                src_ref=a_src.at[step, g], dst_ref=a_recv.at[step, g, col],
                send_sem=a_ss.at[step], recv_sem=a_rs.at[step, g],
                device_id=plane_peer(s)[0], device_id_type=MESH,
            ).start()

    def first_chunk(g):
        found = []
        for q in range(CHUNK):
            r = g * CHUNK + q
            in_copy(r).wait()
            halves = []
            for i in (0, HALF):
                turned = [cost[r, k, i:i + HALF, :].T for k in range(KK)]
                low = None
                for k in range(KK):
                    cost_t[r, k, :, i:i + HALF] = turned[k]
                    v = jnp.min(turned[k].reshape(BS // 16, 16, HALF), axis=0)
                    low = v if low is None else jnp.minimum(low, v)
                low = jnp.min(low.astype(F32), axis=0, keepdims=True) * SCALE
                total = None
                for k in range(KK):
                    p = jnp.exp2(low - turned[k].astype(F32) * SCALE)
                    p = jnp.sum(p.reshape(BS // 8, 8, HALF), axis=0)
                    total = p if total is None else total + p
                halves.append(jnp.log2(jnp.sum(total, axis=0, keepdims=True)) - low)
            found.append(jnp.concatenate(halves, axis=1))
        keep_chunk(0, g, jnp.concatenate(found, axis=0))

    def first_rows(g, _):
        first_chunk(g)
        return 0

    def first_rows_sent(g, _):
        first_chunk(g)
        send_chunk(0, g)
        return 0

    tables()
    lax.fori_loop(0, 2, first_rows, 0)
    pl.semaphore_wait(barrier, PLANE - 1 + NZ - 1)
    send_chunk(0, 0)
    send_chunk(0, 1)
    lax.fori_loop(2, CHUNKS, first_rows_sent, 0)

    def scale_costs(r, _):
        for k in range(KK):
            for i in range(0, BS, SLAB):
                c2[r, k, i:i + SLAB] = cost[r, k, i:i + SLAB].astype(F32) * SCALE
        return 0

    lax.fori_loop(0, ROWS, scale_costs, 0)

    def scale_turned(r, _):
        for k in range(KK):
            for i in range(0, BS, SLAB):
                c2_t[r, k, i:i + SLAB] = cost_t[r, k, i:i + SLAB].astype(F32) * SCALE
        return 0

    def gather(step, h):
        for e in range(ENT):
            c = cand(e)
            gath[e // 8, e % 8:e % 8 + 1, :] = t_recv[step - 1][h][c // 8, pl.ds(c % 8, 1), :]
        for g in range(CHUNKS):
            gath_t[h, g] = gath[g].T

    def source_half(g, h):
        js = slice(h * HALF, (h + 1) * HALF)
        for q in range(CHUNK):
            r = g * CHUNK + q
            wide = [jnp.broadcast_to(gath_t[h, g, :, q * KK + k:q * KK + k + 1], (HALF, HALF)) for k in range(KK)]
            wide_b = [(w * UNSCALE).astype(BF16) for w in wide]
            for i in (0, HALF):
                top = None
                for k in range(KK):
                    v = wide_b[k] - cost_t[r, k, js, i:i + HALF]
                    v = jnp.max(v.reshape(HALF // 16, 16, HALF), axis=0)
                    top = v if top is None else jnp.maximum(top, v)
                top = jnp.max(top.astype(F32), axis=0, keepdims=True) * SCALE
                total = None
                for k in range(KK):
                    for j in range(0, HALF, SLAB):
                        v = (wide[k][j:j + SLAB] - top) - c2_t[r, k, h * HALF + j:h * HALF + j + SLAB, i:i + HALF]
                        p = jnp.sum(jnp.exp2(v).reshape(SLAB // 8, 8, HALF), axis=0)
                        total = p if total is None else total + p
                m2[h, g, q:q + 1, i:i + HALF] = top
                s2[h, g, q:q + 1, i:i + HALF] = jnp.sum(total, axis=0, keepdims=True)

    def both_halves(g):
        top = jnp.maximum(m2[0, g], m2[1, g])
        total = s2[0, g] * jnp.exp2(m2[0, g] - top) + s2[1, g] * jnp.exp2(m2[1, g] - top)
        return top + jnp.log2(total)

    def take_chunk(step, g):
        landed(a_recv.at[step, g], NCOL - 1, a_rs.at[step, g])
        source = slm[g] - lse2(a_recv[step, g])
        if step == ITERS - 1:
            spot[g] = source * UNSCALE
        st[g] = jnp.concatenate([source, jnp.zeros_like(source)], axis=0).T

    def target_part(g, halves):
        for q in range(CHUNK):
            r = g * CHUNK + q
            wide = jnp.broadcast_to(st[g, :, q:q + 1], (BS, HALF))
            wide_b = (wide * UNSCALE).astype(BF16)
            for k in range(KK):
                for h in halves:
                    js = slice(h * HALF, (h + 1) * HALF)
                    v = wide_b - cost[r, k, :, js]
                    v = jnp.max(v.reshape(BS // 16, 16, HALF), axis=0)
                    top = jnp.max(v.astype(F32), axis=0, keepdims=True) * SCALE
                    total = None
                    for i in range(0, BS, SLAB):
                        v = (wide[i:i + SLAB] - top) - c2[r, k, i:i + SLAB, js]
                        p = jnp.sum(jnp.exp2(v).reshape(SLAB // 8, 8, HALF), axis=0)
                        total = p if total is None else total + p
                    j = q * KK + k
                    ment[h, g, j:j + 1, :] = top
                    sent[h, g, j:j + 1, :] = jnp.sum(total, axis=0, keepdims=True)

    def scatter(step, h):
        entries = (ment[h] + jnp.log2(sent[h])).reshape(ENT, HALF)
        blocks = named[...]
        peak = jnp.full((ENT, HALF), LOWEST, F32)
        for e in range(ENT):
            peak = jnp.maximum(peak, jnp.where(blocks == cand(e), entries[e:e + 1], LOWEST))
        shares = jnp.exp2(entries - peak)
        mass = jnp.zeros((ENT, HALF), F32)
        for e in range(ENT):
            mass = mass + jnp.where(blocks == cand(e), shares[e:e + 1], 0.0)
        merged = peak + jnp.log2(mass)
        first = merged.astype(BF16)
        rest = merged - first.astype(F32)
        second = rest.astype(BF16)
        third = (rest - second.astype(F32)).astype(BF16)
        pieces = jnp.concatenate([first, second, third, jnp.zeros_like(third)], axis=0)
        spread = jnp.dot(onehot[...], pieces, preferred_element_type=F32) + missing[...]
        dense[step, h] = spread.reshape(PLANE, 8, HALF)
        r_recv[step, h, me] = dense[step, h, me]

        for s in FAR_PLANE:
            peer, index = plane_peer(s)
            pltpu.make_async_remote_copy(
                src_ref=dense.at[step, h, index], dst_ref=r_recv.at[step, h, me],
                send_sem=r_ss.at[step, h], recv_sem=r_rs.at[step, h],
                device_id=peer, device_id_type=MESH,
            ).start()

    def along_z(step, h):
        landed(r_recv.at[step, h], PLANE - 1, r_rs.at[step, h])
        part = lse2(r_recv[step, h])
        z_src[step, h] = part
        z_recv[step, h, z] = part

        for s in FAR_Z:
            pltpu.make_async_remote_copy(
                src_ref=z_src.at[step, h], dst_ref=z_recv.at[step, h, z],
                send_sem=z_ss.at[step, h], recv_sem=z_rs.at[step, h],
                device_id=z_peer(s), device_id_type=MESH,
            ).start()

    def spread_target(step, h):
        landed(z_recv.at[step, h], NZ - 1, z_rs.at[step, h])
        target = tlm[:, h * HALF:(h + 1) * HALF] * LOG2E - lse2(z_recv[step, h])
        t_src[step, h] = target
        t_recv[step][h][me] = target

        for s in FAR_PLANE:
            pltpu.make_async_remote_copy(
                src_ref=t_src.at[step, h], dst_ref=t_recv[step][h].at[me],
                send_sem=t_ss.at[step, h], recv_sem=t_rs.at[step, h],
                device_id=plane_peer(s)[0], device_id_type=MESH,
            ).start()

    for step in range(ITERS):
        if step > 0:
            for h in range(2):
                landed(t_recv[step - 1][h], PLANE - 1, t_rs.at[step - 1, h])
                gather(step, h)

                def source_rows(g, _):
                    source_half(g, h)
                    if h == 1:
                        keep_chunk(step, g, both_halves(g))
                        send_chunk(step, g)
                    return 0

                lax.fori_loop(0, CHUNKS, source_rows, 0)

        def target_rows(g, _):
            take_chunk(step, g)
            target_part(g, (0, 1))
            return 0

        lax.fori_loop(0, CHUNKS - 1, target_rows, 0)
        take_chunk(step, CHUNKS - 1)
        target_part(CHUNKS - 1, (0,))
        scatter(step, 0)
        target_part(CHUNKS - 1, (1,))
        scatter(step, 1)
        if step == 0:
            tlm_copy().wait()
            lax.fori_loop(0, ROWS, scale_turned, 0)
        along_z(step, 0)
        along_z(step, 1)
        spread_target(step, 0)
        spread_target(step, 1)

    for g in range(CHUNKS):
        src_out[g * CHUNK:(g + 1) * CHUNK] = spot[g]
    for h in range(2):
        landed(t_recv[ITERS - 1][h], PLANE - 1, t_rs.at[ITERS - 1, h])
        tgt_out[:, h * HALF:(h + 1) * HALF] = t_recv[ITERS - 1][h][...].reshape(PLANE * 8, HALF) * UNSCALE

    for step in range(ITERS):
        ref = a_recv.at[step, :, pl.ds(0, NCOL - 1)]
        pltpu.make_async_copy(ref, ref, a_ss.at[step]).wait()
        for h in range(2):
            landed(r_recv.at[step, h], PLANE - 1, r_ss.at[step, h])
            landed(z_recv.at[step, h], NZ - 1, z_ss.at[step, h])
            landed(t_recv[step][h], PLANE - 1, t_ss.at[step, h])


def hand_over(source, target, src_out, tgt_out, held_s, held_t, in_sem, out_sem):
    ways = [(source, held_s, src_out)]
    size = target.shape[0] // PIECES
    for i in range(PIECES):
        part = pl.ds(i * size, size)
        ways.append((target.at[part], held_t.at[part], tgt_out.at[part]))
    ins = [pltpu.make_async_copy(a, v, in_sem.at[i]) for i, (a, v, _) in enumerate(ways)]
    outs = [pltpu.make_async_copy(v, b, out_sem.at[i]) for i, (_, v, b) in enumerate(ways)]
    for c in ins:
        c.start()
    for c, d in zip(ins, outs):
        c.wait()
        d.start()
    for d in outs:
        d.wait()


def per_device(block_cost, candidates, source_logmass, target_logmass):
    vmem = pl.BlockSpec(memory_space=pltpu.VMEM)
    hbm = pl.BlockSpec(memory_space=pl.ANY)
    dma = pltpu.SemaphoreType.DMA
    scratch = [
        ((ROWS, KK, BS, BS), BF16),
        ((ROWS, KK, BS, BS), F32),
        ((ROWS, KK, BS, BS), BF16),
        ((ROWS, KK, BS, BS), F32),
        ((8, BS), F32),
        ((CHUNKS, CHUNK, BS), F32),
        ((CHUNKS, CHUNK, BS), F32),
        ((CHUNKS, BS, 8), F32),
        ((ENT // 8, 8, HALF), F32),
        ((2, CHUNKS, HALF, 8), F32),
        ((2, CHUNKS, CHUNK, BS), F32),
        ((2, CHUNKS, CHUNK, BS), F32),
        ((2, ENT // 8, 8, HALF), F32),
        ((2, ENT // 8, 8, HALF), F32),
        ((ENT, HALF), jnp.int32),
        ((BS, HALF), BF16),
        ((BS, HALF), F32),
        ((ITERS, CHUNKS, CHUNK, BS), F32),
        ((ITERS, CHUNKS, NCOL, CHUNK, BS), F32),
        ((ITERS, 2, PLANE, 8, HALF), F32),
        ((ITERS, 2, PLANE, 8, HALF), F32),
        ((ITERS, 2, 8, HALF), F32),
        ((ITERS, 2, NZ, 8, HALF), F32),
        ((ITERS, 2, 8, HALF), F32),
    ] + [((PLANE, 8, HALF), F32)] * (2 * ITERS)
    source, target = pl.pallas_call(
        body,
        name="sinkhorn",
        out_shape=(
            jax.ShapeDtypeStruct(source_logmass.shape, F32),
            jax.ShapeDtypeStruct(target_logmass.shape, F32),
        ),
        in_specs=[pl.BlockSpec(memory_space=pltpu.SMEM), hbm, vmem, hbm],
        out_specs=(vmem, vmem),
        scratch_shapes=[pltpu.VMEM(*s) for s in scratch]
        + [dma((ROWS + 1,)), dma((ITERS,)), dma((ITERS, CHUNKS))]
        + [dma((ITERS, 2))] * 6,
        compiler_params=pltpu.CompilerParams(
            collective_id=0, has_side_effects=True, vmem_limit_bytes=60 << 20
        ),
    )(candidates.T, block_cost, source_logmass, target_logmass)
    return pl.pallas_call(
        hand_over,
        name="hand_over",
        out_shape=(
            jax.ShapeDtypeStruct(source_logmass.shape, F32),
            jax.ShapeDtypeStruct(target_logmass.shape, F32),
        ),
        in_specs=[hbm, hbm],
        out_specs=(hbm, hbm),
        scratch_shapes=[
            pltpu.VMEM(source_logmass.shape, F32),
            pltpu.VMEM(target_logmass.shape, F32),
            dma((PIECES + 1,)),
            dma((PIECES + 1,)),
        ],
    )(source, target)


def solution(mesh):
    return jax.shard_map(
        per_device,
        mesh=mesh,
        in_specs=(P("row", "col", None, None), P("row", "col"), P("row", None), P()),
        out_specs=(P("row", None), P()),
        check_vma=False,
    )
```

```python
import math

import jax
import jax.numpy as jnp
from jax import lax
from jax.experimental import pallas as pl
from jax.experimental.pallas import tpu as pltpu
from jax.sharding import PartitionSpec as P

ITERS = 2
EPS = 0.05
LOG2E = math.log2(math.e)
SCALE = LOG2E / EPS
UNSCALE = EPS / LOG2E
LOWEST = -1e30
MESH = pl.DeviceIdType.MESH
NX, NY, NZ, NC = 4, 4, 8, 2
PLANE = NX * NY * NC
NCOL = NY * NC
ROWS, KK, BS = 16, 2, 256
ENT = ROWS * KK
HALF = 128
CHUNK = 4
CHUNKS = ROWS // CHUNK
SLAB = 64
PIECES = 4
F32, BF16 = jnp.float32, jnp.bfloat16


def lse2(parts):
    top = jnp.max(parts, axis=0)
    return top + jnp.log2(jnp.sum(jnp.exp2(parts - top[None]), axis=0))


def body(
    cand_ref, cost_hbm, slm_ref, tlm_hbm, src_out, tgt_out,
    cost, c2, cost_t, c2_t, tlm, slm, spot, held, st, gath, gath_t, m2, s2,
    ment, sent, named, onehot, missing,
    a_src, a_recv, dense, r_recv, z_src, z_recv, t_src, t_recv0, t_recv1,
    in_sem, out_sem, a_ss, a_rs, r_ss, r_rs, z_ss, z_rs, t_ss, t_rs,
):
    t_recv = ((t_recv0, t_recv1), (tgt_out.at[0], tgt_out.at[1]))
    row, col = lax.axis_index("row"), lax.axis_index("col")
    z, x = row // NX, row % NX
    y, co = col // NC, col % NC
    me = x * NCOL + col

    def wrap(v, n):
        return jnp.where(v >= n, v - n, v)

    xs = [wrap(x + d, NX) for d in range(NX)]
    ys = [wrap(y + d, NY) for d in range(NY)]
    cs = [co, 1 - co]
    zrows = [wrap(z + d, NZ) * NX + x for d in range(NZ)]
    xrows = [z * NX + v for v in xs]
    cols = [v * NC + c for v in ys for c in cs]

    def hops(s):
        return min(s // NCOL, NX - s // NCOL) + min(s % NCOL // NC, NY - s % NCOL // NC)

    FAR_PLANE = sorted(range(1, PLANE), key=lambda s: -hops(s))
    FAR_COL = sorted(range(1, NCOL), key=lambda s: -hops(s))
    FAR_Z = sorted(range(1, NZ), key=lambda s: -min(s, NZ - s))

    def plane_peer(s):
        return (xrows[s // NCOL], cols[s % NCOL]), xs[s // NCOL] * NCOL + cols[s % NCOL]

    def z_peer(s):
        return (zrows[s], col)

    def in_copy(r):
        return pltpu.make_async_copy(cost_hbm.at[r], cost.at[r], in_sem.at[r])

    def tlm_copy():
        return pltpu.make_async_copy(tlm_hbm.at[pl.ds(me * 8, 8)], tlm, in_sem.at[ROWS])

    for r in range(ROWS):
        in_copy(r).start()
    barrier = pltpu.get_barrier_semaphore()
    for s in FAR_Z:
        pl.semaphore_signal(barrier, inc=1, device_id=z_peer(s), device_id_type=MESH)
    for s in FAR_PLANE:
        pl.semaphore_signal(barrier, inc=1, device_id=plane_peer(s)[0], device_id_type=MESH)
    tlm_copy().start()

    def landed(buf, n, sem):
        ref = buf.at[pl.ds(0, n)]
        pltpu.make_async_copy(ref, ref, sem).wait()

    def cand(e):
        return cand_ref[e % KK, e // KK]

    def tables():
        for g in range(CHUNKS):
            slm[g] = slm_ref[g * CHUNK:(g + 1) * CHUNK] * LOG2E

        sub32 = lax.broadcasted_iota(jnp.int32, (ENT, HALF), 0)
        lane32 = lax.broadcasted_iota(jnp.int32, (ENT, HALF), 1)
        lane8 = lax.broadcasted_iota(jnp.int32, (8, HALF), 1)
        in_lane = jnp.full((8, HALF), -1, jnp.int32)
        in_row = jnp.zeros((ENT, HALF), jnp.int32)
        for e in range(ENT):
            c = cand(e)
            in_lane = jnp.where(lane8 % ENT == e, c, in_lane)
            in_row = jnp.where(sub32 == e, c, in_row)
        named[...] = in_row
        earlier = jnp.max(
            jnp.where((sub32 < lane32 % ENT) & (in_row == jnp.broadcast_to(in_lane[0:1], (ENT, HALF))), 1.0, 0.0),
            axis=0, keepdims=True)
        in_lane = jnp.where(lane8 < 3 * ENT, in_lane, -1)[0:1]
        sub = lax.broadcasted_iota(jnp.int32, (BS, HALF), 0)
        hot = jnp.where(sub == jnp.broadcast_to(in_lane, (BS, HALF)), 1.0, 0.0)
        hot = hot * (1.0 - jnp.broadcast_to(earlier, (BS, HALF)))
        onehot[...] = hot.astype(BF16)
        absent = jnp.where(jnp.sum(hot, axis=1, keepdims=True) > 0.5, 0.0, LOWEST)
        missing[...] = jnp.broadcast_to(absent, (BS, HALF))

    def keep_chunk(step, g, part):
        a_src[step, g] = part
        a_recv[step, g, col] = part

    def send_chunk(step, g):
        for s in FAR_COL:
            pltpu.make_async_remote_copy(
                src_ref=a_src.at[step, g], dst_ref=a_recv.at[step, g, col],
                send_sem=a_ss.at[step], recv_sem=a_rs.at[step, g],
                device_id=plane_peer(s)[0], device_id_type=MESH,
            ).start()

    def first_chunk(g):
        found = []
        for q in range(CHUNK):
            in_copy(g * CHUNK + q).wait()
        for q in range(CHUNK):
            r = g * CHUNK + q
            halves = []
            for i in (0, HALF):
                turned = [cost[r, k, i:i + HALF, :].T for k in range(KK)]
                low = None
                for k in range(KK):
                    cost_t[r, k, :, i:i + HALF] = turned[k]
                    v = jnp.min(turned[k].reshape(BS // 16, 16, HALF), axis=0)
                    low = v if low is None else jnp.minimum(low, v)
                low = jnp.min(low.astype(F32), axis=0, keepdims=True) * SCALE
                total = None
                for k in range(KK):
                    p = jnp.exp2(low - turned[k].astype(F32) * SCALE)
                    p = jnp.sum(p.reshape(BS // 8, 8, HALF), axis=0)
                    total = p if total is None else total + p
                halves.append(jnp.log2(jnp.sum(total, axis=0, keepdims=True)) - low)
            found.append(jnp.concatenate(halves, axis=1))
        keep_chunk(0, g, jnp.concatenate(found, axis=0))

    def first_rows(g, _):
        first_chunk(g)
        return 0

    def first_rows_sent(g, _):
        first_chunk(g)
        send_chunk(0, g)
        return 0

    tables()
    lax.fori_loop(0, 2, first_rows, 0)
    pl.semaphore_wait(barrier, PLANE - 1 + NZ - 1)
    send_chunk(0, 0)
    send_chunk(0, 1)
    lax.fori_loop(2, CHUNKS, first_rows_sent, 0)

    def scale_costs(r, _):
        for k in range(KK):
            for i in range(0, BS, SLAB):
                c2[r, k, i:i + SLAB] = cost[r, k, i:i + SLAB].astype(F32) * SCALE
        return 0

    lax.fori_loop(0, ROWS, scale_costs, 0)

    def scale_turned(r, _):
        for k in range(KK):
            for i in range(0, BS, SLAB):
                c2_t[r, k, i:i + SLAB] = cost_t[r, k, i:i + SLAB].astype(F32) * SCALE
        return 0

    def gather(step, h):
        for e in range(ENT):
            c = cand(e)
            gath[e // 8, e % 8:e % 8 + 1, :] = t_recv[step - 1][h][c // 8, pl.ds(c % 8, 1), :]
        for g in range(CHUNKS):
            gath_t[h, g] = gath[g].T

    def source_half(g, h):
        js = slice(h * HALF, (h + 1) * HALF)
        for q in range(CHUNK):
            r = g * CHUNK + q
            wide = [jnp.broadcast_to(gath_t[h, g, :, q * KK + k:q * KK + k + 1], (HALF, HALF)) for k in range(KK)]
            wide_b = [(w * UNSCALE).astype(BF16) for w in wide]
            for i in (0, HALF):
                top = None
                for k in range(KK):
                    v = wide_b[k] - cost_t[r, k, js, i:i + HALF]
                    v = jnp.max(v.reshape(HALF // 16, 16, HALF), axis=0)
                    top = v if top is None else jnp.maximum(top, v)
                top = jnp.max(top.astype(F32), axis=0, keepdims=True) * SCALE
                total = None
                for k in range(KK):
                    for j in range(0, HALF, SLAB):
                        v = (wide[k][j:j + SLAB] - top) - c2_t[r, k, h * HALF + j:h * HALF + j + SLAB, i:i + HALF]
                        p = jnp.sum(jnp.exp2(v).reshape(SLAB // 8, 8, HALF), axis=0)
                        total = p if total is None else total + p
                m2[h, g, q:q + 1, i:i + HALF] = top
                s2[h, g, q:q + 1, i:i + HALF] = jnp.sum(total, axis=0, keepdims=True)

    def both_halves(g):
        top = jnp.maximum(m2[0, g], m2[1, g])
        total = s2[0, g] * jnp.exp2(m2[0, g] - top) + s2[1, g] * jnp.exp2(m2[1, g] - top)
        return top + jnp.log2(total)

    def take_chunk(step, g):
        landed(a_recv.at[step, g], NCOL - 1, a_rs.at[step, g])
        source = slm[g] - lse2(a_recv[step, g])
        if step == ITERS - 1:
            spot[g] = source * UNSCALE
        st[g] = jnp.concatenate([source, jnp.zeros_like(source)], axis=0).T

    def target_part(g, halves):
        for q in range(CHUNK):
            r = g * CHUNK + q
            wide = jnp.broadcast_to(st[g, :, q:q + 1], (BS, HALF))
            wide_b = (wide * UNSCALE).astype(BF16)
            for k in range(KK):
                for h in halves:
                    js = slice(h * HALF, (h + 1) * HALF)
                    v = wide_b - cost[r, k, :, js]
                    v = jnp.max(v.reshape(BS // 16, 16, HALF), axis=0)
                    top = jnp.max(v.astype(F32), axis=0, keepdims=True) * SCALE
                    total = None
                    for i in range(0, BS, SLAB):
                        v = (wide[i:i + SLAB] - top) - c2[r, k, i:i + SLAB, js]
                        p = jnp.sum(jnp.exp2(v).reshape(SLAB // 8, 8, HALF), axis=0)
                        total = p if total is None else total + p
                    j = q * KK + k
                    ment[h, g, j:j + 1, :] = top
                    sent[h, g, j:j + 1, :] = jnp.sum(total, axis=0, keepdims=True)

    def scatter(step, h):
        entries = (ment[h] + jnp.log2(sent[h])).reshape(ENT, HALF)
        blocks = named[...]
        peak = jnp.full((ENT, HALF), LOWEST, F32)
        for e in range(ENT):
            peak = jnp.maximum(peak, jnp.where(blocks == cand(e), entries[e:e + 1], LOWEST))
        shares = jnp.exp2(entries - peak)
        mass = jnp.zeros((ENT, HALF), F32)
        for e in range(ENT):
            mass = mass + jnp.where(blocks == cand(e), shares[e:e + 1], 0.0)
        merged = peak + jnp.log2(mass)
        first = merged.astype(BF16)
        rest = merged - first.astype(F32)
        second = rest.astype(BF16)
        third = (rest - second.astype(F32)).astype(BF16)
        pieces = jnp.concatenate([first, second, third, jnp.zeros_like(third)], axis=0)
        spread = jnp.dot(onehot[...], pieces, preferred_element_type=F32) + missing[...]
        dense[step, h] = spread.reshape(PLANE, 8, HALF)
        r_recv[step, h, me] = dense[step, h, me]

        for s in FAR_PLANE:
            peer, index = plane_peer(s)
            pltpu.make_async_remote_copy(
                src_ref=dense.at[step, h, index], dst_ref=r_recv.at[step, h, me],
                send_sem=r_ss.at[step, h], recv_sem=r_rs.at[step, h],
                device_id=peer, device_id_type=MESH,
            ).start()

    def along_z(step, h):
        landed(r_recv.at[step, h], PLANE - 1, r_rs.at[step, h])
        part = lse2(r_recv[step, h])
        z_src[step, h] = part
        z_recv[step, h, z] = part

        for s in FAR_Z:
            pltpu.make_async_remote_copy(
                src_ref=z_src.at[step, h], dst_ref=z_recv.at[step, h, z],
                send_sem=z_ss.at[step, h], recv_sem=z_rs.at[step, h],
                device_id=z_peer(s), device_id_type=MESH,
            ).start()

    def own_copy(h):
        return pltpu.make_async_copy(t_src.at[ITERS - 1, h], tgt_out.at[h, me], out_sem.at[h])

    def source_copy():
        return pltpu.make_async_copy(held, src_out, out_sem.at[2])

    def spread_target(step, h):
        landed(z_recv.at[step, h], NZ - 1, z_rs.at[step, h])
        target = tlm[:, h * HALF:(h + 1) * HALF] * LOG2E - lse2(z_recv[step, h])
        if step < ITERS - 1:
            t_src[step, h] = target
            t_recv[step][h][me] = target
        else:
            t_src[step, h] = target * UNSCALE
            own_copy(h).start()

        for s in FAR_PLANE:
            pltpu.make_async_remote_copy(
                src_ref=t_src.at[step, h], dst_ref=t_recv[step][h].at[me],
                send_sem=t_ss.at[step, h], recv_sem=t_rs.at[step, h],
                device_id=plane_peer(s)[0], device_id_type=MESH,
            ).start()

    for step in range(ITERS):
        if step > 0:
            for h in range(2):
                landed(t_recv[step - 1][h], PLANE - 1, t_rs.at[step - 1, h])
                gather(step, h)

                def source_rows(g, _):
                    source_half(g, h)
                    if h == 1:
                        keep_chunk(step, g, both_halves(g))
                        send_chunk(step, g)
                    return 0

                lax.fori_loop(0, CHUNKS, source_rows, 0)

        def target_rows(g, _):
            take_chunk(step, g)
            target_part(g, (0, 1))
            return 0

        lax.fori_loop(0, CHUNKS - 1, target_rows, 0)
        take_chunk(step, CHUNKS - 1)
        target_part(CHUNKS - 1, (0,))
        scatter(step, 0)
        target_part(CHUNKS - 1, (1,))
        scatter(step, 1)
        if step == 0:
            tlm_copy().wait()
            lax.fori_loop(0, ROWS, scale_turned, 0)
        if step == ITERS - 1:
            for g in range(CHUNKS):
                held[g * CHUNK:(g + 1) * CHUNK] = spot[g]
            source_copy().start()
        along_z(step, 0)
        along_z(step, 1)
        spread_target(step, 0)
        spread_target(step, 1)

    for h in range(2):
        landed(t_recv[ITERS - 1][h], PLANE - 1, t_rs.at[ITERS - 1, h])
        own_copy(h).wait()
    source_copy().wait()

    for step in range(ITERS):
        ref = a_recv.at[step, :, pl.ds(0, NCOL - 1)]
        pltpu.make_async_copy(ref, ref, a_ss.at[step]).wait()
        for h in range(2):
            landed(r_recv.at[step, h], PLANE - 1, r_ss.at[step, h])
            landed(z_recv.at[step, h], NZ - 1, z_ss.at[step, h])
            landed(t_recv[step][h], PLANE - 1, t_ss.at[step, h])


def hand_over(source, target, src_out, tgt_out, held_s, held_t, in_sem, out_sem):
    ways = [(source, held_s, src_out)]
    size = tgt_out.shape[0] * 2 // PIECES
    for i in range(PIECES):
        h, first = i % 2, i // 2 * size
        part = pl.ds(first, size)
        ways.append((
            target.at[h, part], held_t.at[h, part], tgt_out.at[part, pl.ds(h * HALF, HALF)]
        ))
    ins = [pltpu.make_async_copy(a, v, in_sem.at[i]) for i, (a, v, _) in enumerate(ways)]
    outs = [pltpu.make_async_copy(v, b, out_sem.at[i]) for i, (_, v, b) in enumerate(ways)]
    for c in ins:
        c.start()
    for c, d in zip(ins, outs):
        c.wait()
        d.start()
    for d in outs:
        d.wait()


def per_device(block_cost, candidates, source_logmass, target_logmass):
    vmem = pl.BlockSpec(memory_space=pltpu.VMEM)
    hbm = pl.BlockSpec(memory_space=pl.ANY)
    dma = pltpu.SemaphoreType.DMA
    scratch = [
        ((ROWS, KK, BS, BS), BF16),
        ((ROWS, KK, BS, BS), F32),
        ((ROWS, KK, BS, BS), BF16),
        ((ROWS, KK, BS, BS), F32),
        ((8, BS), F32),
        ((CHUNKS, CHUNK, BS), F32),
        ((CHUNKS, CHUNK, BS), F32),
        ((ROWS, BS), F32),
        ((CHUNKS, BS, 8), F32),
        ((ENT // 8, 8, HALF), F32),
        ((2, CHUNKS, HALF, 8), F32),
        ((2, CHUNKS, CHUNK, BS), F32),
        ((2, CHUNKS, CHUNK, BS), F32),
        ((2, ENT // 8, 8, HALF), F32),
        ((2, ENT // 8, 8, HALF), F32),
        ((ENT, HALF), jnp.int32),
        ((BS, HALF), BF16),
        ((BS, HALF), F32),
        ((ITERS, CHUNKS, CHUNK, BS), F32),
        ((ITERS, CHUNKS, NCOL, CHUNK, BS), F32),
        ((ITERS, 2, PLANE, 8, HALF), F32),
        ((ITERS, 2, PLANE, 8, HALF), F32),
        ((ITERS, 2, 8, HALF), F32),
        ((ITERS, 2, NZ, 8, HALF), F32),
        ((ITERS, 2, 8, HALF), F32),
    ] + [((PLANE, 8, HALF), F32)] * 2
    source, target = pl.pallas_call(
        body,
        name="sinkhorn",
        out_shape=(
            jax.ShapeDtypeStruct(source_logmass.shape, F32),
            jax.ShapeDtypeStruct((2, PLANE, 8, HALF), F32),
        ),
        in_specs=[pl.BlockSpec(memory_space=pltpu.SMEM), hbm, vmem, hbm],
        out_specs=(hbm, hbm),
        scratch_shapes=[pltpu.VMEM(*s) for s in scratch]
        + [dma((ROWS + 1,)), dma((3,)), dma((ITERS,)), dma((ITERS, CHUNKS))]
        + [dma((ITERS, 2))] * 6,
        compiler_params=pltpu.CompilerParams(
            collective_id=0, has_side_effects=True, vmem_limit_bytes=60 << 20
        ),
    )(candidates.T, block_cost, source_logmass, target_logmass)
    return pl.pallas_call(
        hand_over,
        name="hand_over",
        out_shape=(
            jax.ShapeDtypeStruct(source_logmass.shape, F32),
            jax.ShapeDtypeStruct(target_logmass.shape, F32),
        ),
        in_specs=[hbm, hbm],
        out_specs=(hbm, hbm),
        scratch_shapes=[
            pltpu.VMEM(source_logmass.shape, F32),
            pltpu.VMEM((2, PLANE * 8, HALF), F32),
            dma((PIECES + 1,)),
            dma((PIECES + 1,)),
        ],
    )(source, target.reshape(2, PLANE * 8, HALF))


def solution(mesh):
    return jax.shard_map(
        per_device,
        mesh=mesh,
        in_specs=(P("row", "col", None, None), P("row", "col"), P("row", None), P()),
        out_specs=(P("row", None), P()),
        check_vma=False,
    )
```

```python
import math

import jax
import jax.numpy as jnp
from jax import lax
from jax.experimental import pallas as pl
from jax.experimental.pallas import tpu as pltpu
from jax.sharding import PartitionSpec as P

ITERS = 2
EPS = 0.05
LOG2E = math.log2(math.e)
SCALE = LOG2E / EPS
UNSCALE = EPS / LOG2E
LOWEST = -1e30
MESH = pl.DeviceIdType.MESH
NX, NY, NZ, NC = 4, 4, 8, 2
PLANE = NX * NY * NC
NCOL = NY * NC
ROWS, KK, BS = 16, 2, 256
ENT = ROWS * KK
HALF = 128
CHUNK = 4
CHUNKS = ROWS // CHUNK
SLAB = 64
PIECES = 4
F32, BF16 = jnp.float32, jnp.bfloat16


def lse2(parts):
    top = jnp.max(parts, axis=0)
    return top + jnp.log2(jnp.sum(jnp.exp2(parts - top[None]), axis=0))


def body(
    cand_ref, cost_hbm, slm_ref, tlm_hbm, src_out, tgt_out,
    cost, c2, cost_t, c2_t, tlm, slm, spot, held, st, gath, gath_t, m2, s2,
    ment, sent, named, onehot, missing,
    a_src, a_recv, dense, r_recv, z_src, z_recv, t_src, t_recv0, t_recv1,
    in_sem, out_sem, a_ss, a_rs, r_ss, r_rs, z_ss, z_rs, t_ss, t_rs,
):
    t_recv = ((t_recv0, t_recv1), (tgt_out.at[0], tgt_out.at[1]))
    row, col = lax.axis_index("row"), lax.axis_index("col")
    z, x = row // NX, row % NX
    y, co = col // NC, col % NC
    me = x * NCOL + col

    def wrap(v, n):
        return jnp.where(v >= n, v - n, v)

    xs = [wrap(x + d, NX) for d in range(NX)]
    ys = [wrap(y + d, NY) for d in range(NY)]
    cs = [co, 1 - co]
    zrows = [wrap(z + d, NZ) * NX + x for d in range(NZ)]
    xrows = [z * NX + v for v in xs]
    cols = [v * NC + c for v in ys for c in cs]

    def hops(s):
        return min(s // NCOL, NX - s // NCOL) + min(s % NCOL // NC, NY - s % NCOL // NC)

    FAR_PLANE = sorted(range(1, PLANE), key=lambda s: -hops(s))
    FAR_COL = sorted(range(1, NCOL), key=lambda s: -hops(s))
    FAR_Z = sorted(range(1, NZ), key=lambda s: -min(s, NZ - s))

    def plane_peer(s):
        return (xrows[s // NCOL], cols[s % NCOL]), xs[s // NCOL] * NCOL + cols[s % NCOL]

    def z_peer(s):
        return (zrows[s], col)

    def in_copy(r):
        return pltpu.make_async_copy(cost_hbm.at[r], cost.at[r], in_sem.at[r])

    def tlm_copy():
        return pltpu.make_async_copy(tlm_hbm.at[pl.ds(me * 8, 8)], tlm, in_sem.at[ROWS])

    for r in range(ROWS):
        in_copy(r).start()
    barrier = pltpu.get_barrier_semaphore()
    for s in FAR_Z:
        pl.semaphore_signal(barrier, inc=1, device_id=z_peer(s), device_id_type=MESH)
    for s in FAR_PLANE:
        pl.semaphore_signal(barrier, inc=1, device_id=plane_peer(s)[0], device_id_type=MESH)
    tlm_copy().start()

    def landed(buf, n, sem):
        ref = buf.at[pl.ds(0, n)]
        pltpu.make_async_copy(ref, ref, sem).wait()

    def cand(e):
        return cand_ref[e % KK, e // KK]

    def tables():
        for g in range(CHUNKS):
            slm[g] = slm_ref[g * CHUNK:(g + 1) * CHUNK] * LOG2E

        sub32 = lax.broadcasted_iota(jnp.int32, (ENT, HALF), 0)
        lane32 = lax.broadcasted_iota(jnp.int32, (ENT, HALF), 1)
        lane8 = lax.broadcasted_iota(jnp.int32, (8, HALF), 1)
        in_lane = jnp.full((8, HALF), -1, jnp.int32)
        in_row = jnp.zeros((ENT, HALF), jnp.int32)
        for e in range(ENT):
            c = cand(e)
            in_lane = jnp.where(lane8 % ENT == e, c, in_lane)
            in_row = jnp.where(sub32 == e, c, in_row)
        named[...] = in_row
        earlier = jnp.max(
            jnp.where((sub32 < lane32 % ENT) & (in_row == jnp.broadcast_to(in_lane[0:1], (ENT, HALF))), 1.0, 0.0),
            axis=0, keepdims=True)
        in_lane = jnp.where(lane8 < 3 * ENT, in_lane, -1)[0:1]
        sub = lax.broadcasted_iota(jnp.int32, (BS, HALF), 0)
        hot = jnp.where(sub == jnp.broadcast_to(in_lane, (BS, HALF)), 1.0, 0.0)
        hot = hot * (1.0 - jnp.broadcast_to(earlier, (BS, HALF)))
        onehot[...] = hot.astype(BF16)
        absent = jnp.where(jnp.sum(hot, axis=1, keepdims=True) > 0.5, 0.0, LOWEST)
        missing[...] = jnp.broadcast_to(absent, (BS, HALF))

    def keep_chunk(step, g, part):
        a_src[step, g] = part
        a_recv[step, g, col] = part

    def send_chunk(step, g):
        for s in FAR_COL:
            pltpu.make_async_remote_copy(
                src_ref=a_src.at[step, g], dst_ref=a_recv.at[step, g, col],
                send_sem=a_ss.at[step], recv_sem=a_rs.at[step, g],
                device_id=plane_peer(s)[0], device_id_type=MESH,
            ).start()

    def first_chunk(g):
        found = []
        for q in range(CHUNK):
            in_copy(g * CHUNK + q).wait()
        for q in range(CHUNK):
            r = g * CHUNK + q
            halves = []
            for i in (0, HALF):
                turned = [cost[r, k, i:i + HALF, :].T for k in range(KK)]
                low = None
                for k in range(KK):
                    cost_t[r, k, :, i:i + HALF] = turned[k]
                    v = jnp.min(turned[k].reshape(BS // 16, 16, HALF), axis=0)
                    low = v if low is None else jnp.minimum(low, v)
                low = jnp.min(low.astype(F32), axis=0, keepdims=True) * SCALE
                total = None
                for k in range(KK):
                    p = jnp.exp2(low - turned[k].astype(F32) * SCALE)
                    p = jnp.sum(p.reshape(BS // 8, 8, HALF), axis=0)
                    total = p if total is None else total + p
                halves.append(jnp.log2(jnp.sum(total, axis=0, keepdims=True)) - low)
            found.append(jnp.concatenate(halves, axis=1))
        keep_chunk(0, g, jnp.concatenate(found, axis=0))

    def first_rows(g, _):
        first_chunk(g)
        return 0

    def first_rows_sent(g, _):
        first_chunk(g)
        send_chunk(0, g)
        return 0

    tables()
    lax.fori_loop(0, 2, first_rows, 0)
    pl.semaphore_wait(barrier, PLANE - 1 + NZ - 1)
    send_chunk(0, 0)
    send_chunk(0, 1)
    lax.fori_loop(2, CHUNKS, first_rows_sent, 0)

    def scale_costs(r, _):
        for k in range(KK):
            for i in range(0, BS, SLAB):
                c2[r, k, i:i + SLAB] = cost[r, k, i:i + SLAB].astype(F32) * SCALE
        return 0

    lax.fori_loop(0, ROWS, scale_costs, 0)

    def scale_turned(r, _):
        for k in range(KK):
            for i in range(0, BS, SLAB):
                c2_t[r, k, i:i + SLAB] = cost_t[r, k, i:i + SLAB].astype(F32) * SCALE
        return 0

    def gather(step, h):
        for e in range(ENT):
            c = cand(e)
            gath[e // 8, e % 8:e % 8 + 1, :] = t_recv[step - 1][h][c // 8, pl.ds(c % 8, 1), :]
        for g in range(CHUNKS):
            gath_t[h, g] = gath[g].T

    def source_half(g, h):
        js = slice(h * HALF, (h + 1) * HALF)
        for q in range(CHUNK):
            r = g * CHUNK + q
            wide = [jnp.broadcast_to(gath_t[h, g, :, q * KK + k:q * KK + k + 1], (HALF, HALF)) for k in range(KK)]
            wide_b = [(w * UNSCALE).astype(BF16) for w in wide]
            for i in (0, HALF):
                top = None
                for k in range(KK):
                    v = wide_b[k] - cost_t[r, k, js, i:i + HALF]
                    v = jnp.max(v.reshape(HALF // 16, 16, HALF), axis=0)
                    top = v if top is None else jnp.maximum(top, v)
                top = jnp.max(top.astype(F32), axis=0, keepdims=True) * SCALE
                total = None
                for k in range(KK):
                    for j in range(0, HALF, SLAB):
                        v = (wide[k][j:j + SLAB] - top) - c2_t[r, k, h * HALF + j:h * HALF + j + SLAB, i:i + HALF]
                        p = jnp.sum(jnp.exp2(v).reshape(SLAB // 8, 8, HALF), axis=0)
                        total = p if total is None else total + p
                m2[h, g, q:q + 1, i:i + HALF] = top
                s2[h, g, q:q + 1, i:i + HALF] = jnp.sum(total, axis=0, keepdims=True)

    def both_halves(g):
        top = jnp.maximum(m2[0, g], m2[1, g])
        total = s2[0, g] * jnp.exp2(m2[0, g] - top) + s2[1, g] * jnp.exp2(m2[1, g] - top)
        return top + jnp.log2(total)

    def take_chunk(step, g):
        landed(a_recv.at[step, g], NCOL - 1, a_rs.at[step, g])
        source = slm[g] - lse2(a_recv[step, g])
        if step == ITERS - 1:
            spot[g] = source * UNSCALE
        st[g] = jnp.concatenate([source, jnp.zeros_like(source)], axis=0).T

    def target_part(g, halves):
        for q in range(CHUNK):
            r = g * CHUNK + q
            wide = jnp.broadcast_to(st[g, :, q:q + 1], (BS, HALF))
            wide_b = (wide * UNSCALE).astype(BF16)
            for k in range(KK):
                for h in halves:
                    js = slice(h * HALF, (h + 1) * HALF)
                    v = wide_b - cost[r, k, :, js]
                    v = jnp.max(v.reshape(BS // 16, 16, HALF), axis=0)
                    top = jnp.max(v.astype(F32), axis=0, keepdims=True) * SCALE
                    total = None
                    for i in range(0, BS, SLAB):
                        v = (wide[i:i + SLAB] - top) - c2[r, k, i:i + SLAB, js]
                        p = jnp.sum(jnp.exp2(v).reshape(SLAB // 8, 8, HALF), axis=0)
                        total = p if total is None else total + p
                    j = q * KK + k
                    ment[h, g, j:j + 1, :] = top
                    sent[h, g, j:j + 1, :] = jnp.sum(total, axis=0, keepdims=True)

    def scatter(step, h):
        entries = (ment[h] + jnp.log2(sent[h])).reshape(ENT, HALF)
        blocks = named[...]
        peak = jnp.full((ENT, HALF), LOWEST, F32)
        for e in range(ENT):
            peak = jnp.maximum(peak, jnp.where(blocks == cand(e), entries[e:e + 1], LOWEST))
        shares = jnp.exp2(entries - peak)
        mass = jnp.zeros((ENT, HALF), F32)
        for e in range(ENT):
            mass = mass + jnp.where(blocks == cand(e), shares[e:e + 1], 0.0)
        merged = peak + jnp.log2(mass)
        first = merged.astype(BF16)
        rest = merged - first.astype(F32)
        second = rest.astype(BF16)
        third = (rest - second.astype(F32)).astype(BF16)
        pieces = jnp.concatenate([first, second, third, jnp.zeros_like(third)], axis=0)
        spread = jnp.dot(onehot[...], pieces, preferred_element_type=F32) + missing[...]
        dense[step, h] = spread.reshape(PLANE, 8, HALF)
        r_recv[step, h, me] = dense[step, h, me]

        for s in FAR_PLANE:
            peer, index = plane_peer(s)
            pltpu.make_async_remote_copy(
                src_ref=dense.at[step, h, index], dst_ref=r_recv.at[step, h, me],
                send_sem=r_ss.at[step, h], recv_sem=r_rs.at[step, h],
                device_id=peer, device_id_type=MESH,
            ).start()

    def along_z(step, h):
        landed(r_recv.at[step, h], PLANE - 1, r_rs.at[step, h])
        part = lse2(r_recv[step, h])
        z_src[step, h] = part
        z_recv[step, h, z] = part

        for s in FAR_Z:
            pltpu.make_async_remote_copy(
                src_ref=z_src.at[step, h], dst_ref=z_recv.at[step, h, z],
                send_sem=z_ss.at[step, h], recv_sem=z_rs.at[step, h],
                device_id=z_peer(s), device_id_type=MESH,
            ).start()

    def own_copy(h):
        return pltpu.make_async_copy(t_src.at[ITERS - 1, h], tgt_out.at[h, me], out_sem.at[h])

    def source_copy():
        return pltpu.make_async_copy(held, src_out, out_sem.at[2])

    def spread_target(step, h):
        landed(z_recv.at[step, h], NZ - 1, z_rs.at[step, h])
        target = tlm[:, h * HALF:(h + 1) * HALF] * LOG2E - lse2(z_recv[step, h])
        if step < ITERS - 1:
            t_src[step, h] = target
            t_recv[step][h][me] = target
        else:
            t_src[step, h] = target * UNSCALE
            own_copy(h).start()

        for s in FAR_PLANE:
            pltpu.make_async_remote_copy(
                src_ref=t_src.at[step, h], dst_ref=t_recv[step][h].at[me],
                send_sem=t_ss.at[step, h], recv_sem=t_rs.at[step, h],
                device_id=plane_peer(s)[0], device_id_type=MESH,
            ).start()

    for step in range(ITERS):
        if step > 0:
            for h in range(2):
                landed(t_recv[step - 1][h], PLANE - 1, t_rs.at[step - 1, h])
                gather(step, h)

                def source_rows(g, _):
                    source_half(g, h)
                    if h == 1:
                        keep_chunk(step, g, both_halves(g))
                        send_chunk(step, g)
                    return 0

                lax.fori_loop(0, CHUNKS, source_rows, 0)

        def target_rows_first(g, _):
            take_chunk(step, g + 1)
            target_part(g, (0,))
            return 0

        def target_rows_second(g, _):
            target_part(g, (1,))
            return 0

        take_chunk(step, 0)
        lax.fori_loop(0, CHUNKS - 1, target_rows_first, 0)
        target_part(CHUNKS - 1, (0,))
        scatter(step, 0)
        lax.fori_loop(0, CHUNKS, target_rows_second, 0)
        scatter(step, 1)
        if step == 0:
            tlm_copy().wait()
            lax.fori_loop(0, ROWS, scale_turned, 0)
        if step == ITERS - 1:
            for g in range(CHUNKS):
                held[g * CHUNK:(g + 1) * CHUNK] = spot[g]
            source_copy().start()
        along_z(step, 0)
        along_z(step, 1)
        spread_target(step, 0)
        spread_target(step, 1)

    for h in range(2):
        landed(t_recv[ITERS - 1][h], PLANE - 1, t_rs.at[ITERS - 1, h])
        own_copy(h).wait()
    source_copy().wait()

    for step in range(ITERS):
        ref = a_recv.at[step, :, pl.ds(0, NCOL - 1)]
        pltpu.make_async_copy(ref, ref, a_ss.at[step]).wait()
        for h in range(2):
            landed(r_recv.at[step, h], PLANE - 1, r_ss.at[step, h])
            landed(z_recv.at[step, h], NZ - 1, z_ss.at[step, h])
            landed(t_recv[step][h], PLANE - 1, t_ss.at[step, h])


def hand_over(source, target, src_out, tgt_out, held_s, held_t, in_sem, out_sem):
    ways = [(source, held_s, src_out)]
    size = tgt_out.shape[0] * 2 // PIECES
    for i in range(PIECES):
        h, first = i % 2, i // 2 * size
        part = pl.ds(first, size)
        ways.append((
            target.at[h, part], held_t.at[h, part], tgt_out.at[part, pl.ds(h * HALF, HALF)]
        ))
    ins = [pltpu.make_async_copy(a, v, in_sem.at[i]) for i, (a, v, _) in enumerate(ways)]
    outs = [pltpu.make_async_copy(v, b, out_sem.at[i]) for i, (_, v, b) in enumerate(ways)]
    for c in ins:
        c.start()
    for c, d in zip(ins, outs):
        c.wait()
        d.start()
    for d in outs:
        d.wait()


def per_device(block_cost, candidates, source_logmass, target_logmass):
    vmem = pl.BlockSpec(memory_space=pltpu.VMEM)
    hbm = pl.BlockSpec(memory_space=pl.ANY)
    dma = pltpu.SemaphoreType.DMA
    scratch = [
        ((ROWS, KK, BS, BS), BF16),
        ((ROWS, KK, BS, BS), F32),
        ((ROWS, KK, BS, BS), BF16),
        ((ROWS, KK, BS, BS), F32),
        ((8, BS), F32),
        ((CHUNKS, CHUNK, BS), F32),
        ((CHUNKS, CHUNK, BS), F32),
        ((ROWS, BS), F32),
        ((CHUNKS, BS, 8), F32),
        ((ENT // 8, 8, HALF), F32),
        ((2, CHUNKS, HALF, 8), F32),
        ((2, CHUNKS, CHUNK, BS), F32),
        ((2, CHUNKS, CHUNK, BS), F32),
        ((2, ENT // 8, 8, HALF), F32),
        ((2, ENT // 8, 8, HALF), F32),
        ((ENT, HALF), jnp.int32),
        ((BS, HALF), BF16),
        ((BS, HALF), F32),
        ((ITERS, CHUNKS, CHUNK, BS), F32),
        ((ITERS, CHUNKS, NCOL, CHUNK, BS), F32),
        ((ITERS, 2, PLANE, 8, HALF), F32),
        ((ITERS, 2, PLANE, 8, HALF), F32),
        ((ITERS, 2, 8, HALF), F32),
        ((ITERS, 2, NZ, 8, HALF), F32),
        ((ITERS, 2, 8, HALF), F32),
    ] + [((PLANE, 8, HALF), F32)] * 2
    source, target = pl.pallas_call(
        body,
        name="sinkhorn",
        out_shape=(
            jax.ShapeDtypeStruct(source_logmass.shape, F32),
            jax.ShapeDtypeStruct((2, PLANE, 8, HALF), F32),
        ),
        in_specs=[pl.BlockSpec(memory_space=pltpu.SMEM), hbm, vmem, hbm],
        out_specs=(hbm, hbm),
        scratch_shapes=[pltpu.VMEM(*s) for s in scratch]
        + [dma((ROWS + 1,)), dma((3,)), dma((ITERS,)), dma((ITERS, CHUNKS))]
        + [dma((ITERS, 2))] * 6,
        compiler_params=pltpu.CompilerParams(
            collective_id=0, has_side_effects=True, vmem_limit_bytes=60 << 20
        ),
    )(candidates.T, block_cost, source_logmass, target_logmass)
    return pl.pallas_call(
        hand_over,
        name="hand_over",
        out_shape=(
            jax.ShapeDtypeStruct(source_logmass.shape, F32),
            jax.ShapeDtypeStruct(target_logmass.shape, F32),
        ),
        in_specs=[hbm, hbm],
        out_specs=(hbm, hbm),
        scratch_shapes=[
            pltpu.VMEM(source_logmass.shape, F32),
            pltpu.VMEM((2, PLANE * 8, HALF), F32),
            dma((PIECES + 1,)),
            dma((PIECES + 1,)),
        ],
    )(source, target.reshape(2, PLANE * 8, HALF))


def solution(mesh):
    return jax.shard_map(
        per_device,
        mesh=mesh,
        in_specs=(P("row", "col", None, None), P("row", "col"), P("row", None), P()),
        out_specs=(P("row", None), P()),
        check_vma=False,
    )
```

```python
import math

import jax
import jax.numpy as jnp
from jax import lax
from jax.experimental import pallas as pl
from jax.experimental.pallas import tpu as pltpu
from jax.sharding import PartitionSpec as P

ITERS = 2
EPS = 0.05
LOG2E = math.log2(math.e)
SCALE = LOG2E / EPS
UNSCALE = EPS / LOG2E
LOWEST = -1e30
MESH = pl.DeviceIdType.MESH
NX, NY, NZ, NC = 4, 4, 8, 2
PLANE = NX * NY * NC
NCOL = NY * NC
ROWS, KK, BS = 16, 2, 256
ENT = ROWS * KK
HALF = 128
CHUNK = 4
CHUNKS = ROWS // CHUNK
SLAB = 64
PIECES = 4
F32, BF16 = jnp.float32, jnp.bfloat16


def lse2(parts):
    top = jnp.max(parts, axis=0)
    return top + jnp.log2(jnp.sum(jnp.exp2(parts - top[None]), axis=0))


def body(
    cand_ref, cost_hbm, slm_ref, tlm_hbm, src_out, tgt_out,
    cost, c2, cost_t, c2_t, tlm, slm, spot, held, st, gath, gath_t, m2, s2,
    ment, sent, named, onehot, missing,
    a_src, a_recv, dense, r_recv, z_src, z_recv, t_src, t_recv0, t_recv1,
    in_sem, out_sem, a_ss, a_rs, r_ss, r_rs, z_ss, z_rs, t_ss, t_rs,
):
    t_recv = ((t_recv0, t_recv1), (tgt_out.at[0], tgt_out.at[1]))
    row, col = lax.axis_index("row"), lax.axis_index("col")
    z, x = row // NX, row % NX
    y, co = col // NC, col % NC
    me = x * NCOL + col

    def wrap(v, n):
        return jnp.where(v >= n, v - n, v)

    xs = [wrap(x + d, NX) for d in range(NX)]
    ys = [wrap(y + d, NY) for d in range(NY)]
    cs = [co, 1 - co]
    zrows = [wrap(z + d, NZ) * NX + x for d in range(NZ)]
    xrows = [z * NX + v for v in xs]
    cols = [v * NC + c for v in ys for c in cs]

    def hops(s):
        return min(s // NCOL, NX - s // NCOL) + min(s % NCOL // NC, NY - s % NCOL // NC)

    FAR_PLANE = sorted(range(1, PLANE), key=lambda s: -hops(s))
    FAR_COL = sorted(range(1, NCOL), key=lambda s: -hops(s))
    FAR_Z = sorted(range(1, NZ), key=lambda s: -min(s, NZ - s))

    def plane_peer(s):
        return (xrows[s // NCOL], cols[s % NCOL]), xs[s // NCOL] * NCOL + cols[s % NCOL]

    def z_peer(s):
        return (zrows[s], col)

    def in_copy(r):
        return pltpu.make_async_copy(cost_hbm.at[r], cost.at[r], in_sem.at[r])

    def tlm_copy():
        return pltpu.make_async_copy(tlm_hbm.at[pl.ds(me * 8, 8)], tlm, in_sem.at[ROWS])

    for r in range(ROWS):
        in_copy(r).start()
    barrier = pltpu.get_barrier_semaphore()
    for s in FAR_Z:
        pl.semaphore_signal(barrier, inc=1, device_id=z_peer(s), device_id_type=MESH)
    for s in FAR_PLANE:
        pl.semaphore_signal(barrier, inc=1, device_id=plane_peer(s)[0], device_id_type=MESH)
    tlm_copy().start()

    def landed(buf, n, sem):
        ref = buf.at[pl.ds(0, n)]
        pltpu.make_async_copy(ref, ref, sem).wait()

    def cand(e):
        return cand_ref[e % KK, e // KK]

    def tables():
        for g in range(CHUNKS):
            slm[g] = slm_ref[g * CHUNK:(g + 1) * CHUNK] * LOG2E

        sub32 = lax.broadcasted_iota(jnp.int32, (ENT, HALF), 0)
        lane32 = lax.broadcasted_iota(jnp.int32, (ENT, HALF), 1)
        lane8 = lax.broadcasted_iota(jnp.int32, (8, HALF), 1)
        in_lane = jnp.full((8, HALF), -1, jnp.int32)
        in_row = jnp.zeros((ENT, HALF), jnp.int32)
        for e in range(ENT):
            c = cand(e)
            in_lane = jnp.where(lane8 % ENT == e, c, in_lane)
            in_row = jnp.where(sub32 == e, c, in_row)
        named[...] = in_row
        earlier = jnp.max(
            jnp.where((sub32 < lane32 % ENT) & (in_row == jnp.broadcast_to(in_lane[0:1], (ENT, HALF))), 1.0, 0.0),
            axis=0, keepdims=True)
        in_lane = jnp.where(lane8 < 3 * ENT, in_lane, -1)[0:1]
        sub = lax.broadcasted_iota(jnp.int32, (BS, HALF), 0)
        hot = jnp.where(sub == jnp.broadcast_to(in_lane, (BS, HALF)), 1.0, 0.0)
        hot = hot * (1.0 - jnp.broadcast_to(earlier, (BS, HALF)))
        onehot[...] = hot.astype(BF16)
        absent = jnp.where(jnp.sum(hot, axis=1, keepdims=True) > 0.5, 0.0, LOWEST)
        missing[...] = jnp.broadcast_to(absent, (BS, HALF))

    def keep_chunk(step, g, part):
        a_src[step, g] = part
        a_recv[step, g, col] = part

    def send_chunk(step, g):
        for s in FAR_COL:
            pltpu.make_async_remote_copy(
                src_ref=a_src.at[step, g], dst_ref=a_recv.at[step, g, col],
                send_sem=a_ss.at[step], recv_sem=a_rs.at[step, g],
                device_id=plane_peer(s)[0], device_id_type=MESH,
            ).start()

    def first_chunk(g):
        found = []
        for q in range(CHUNK):
            in_copy(g * CHUNK + q).wait()
        for q in range(CHUNK):
            r = g * CHUNK + q
            halves = []
            for i in (0, HALF):
                turned = [cost[r, k, i:i + HALF, :].T for k in range(KK)]
                low = None
                for k in range(KK):
                    cost_t[r, k, :, i:i + HALF] = turned[k]
                    v = jnp.min(turned[k].reshape(BS // 16, 16, HALF), axis=0)
                    low = v if low is None else jnp.minimum(low, v)
                low = jnp.min(low.astype(F32), axis=0, keepdims=True) * SCALE
                total = None
                for k in range(KK):
                    p = jnp.exp2(low - turned[k].astype(F32) * SCALE)
                    p = jnp.sum(p.reshape(BS // 8, 8, HALF), axis=0)
                    total = p if total is None else total + p
                halves.append(jnp.log2(jnp.sum(total, axis=0, keepdims=True)) - low)
            found.append(jnp.concatenate(halves, axis=1))
        keep_chunk(0, g, jnp.concatenate(found, axis=0))

    def first_rows(g, _):
        first_chunk(g)
        return 0

    def first_rows_sent(g, _):
        first_chunk(g)
        send_chunk(0, g)
        return 0

    lax.fori_loop(0, CHUNKS, first_rows, 0)
    pl.semaphore_wait(barrier, PLANE - 1 + NZ - 1)
    send_chunk(0, 0)
    send_chunk(0, 1)
    send_chunk(0, 2)
    send_chunk(0, 3)


    def scale_costs(r, _):
        for k in range(KK):
            for i in range(0, BS, SLAB):
                c2[r, k, i:i + SLAB] = cost[r, k, i:i + SLAB].astype(F32) * SCALE
        return 0

    lax.fori_loop(0, ROWS, scale_costs, 0)
    tables()

    def scale_turned(r, _):
        for k in range(KK):
            for i in range(0, BS, SLAB):
                c2_t[r, k, i:i + SLAB] = cost_t[r, k, i:i + SLAB].astype(F32) * SCALE
        return 0

    def gather(step, h):
        for e in range(ENT):
            c = cand(e)
            gath[e // 8, e % 8:e % 8 + 1, :] = t_recv[step - 1][h][c // 8, pl.ds(c % 8, 1), :]
        for g in range(CHUNKS):
            gath_t[h, g] = gath[g].T

    def source_half(g, h):
        js = slice(h * HALF, (h + 1) * HALF)
        for q in range(CHUNK):
            r = g * CHUNK + q
            wide = [jnp.broadcast_to(gath_t[h, g, :, q * KK + k:q * KK + k + 1], (HALF, HALF)) for k in range(KK)]
            wide_b = [(w * UNSCALE).astype(BF16) for w in wide]
            for i in (0, HALF):
                top = None
                for k in range(KK):
                    v = wide_b[k] - cost_t[r, k, js, i:i + HALF]
                    v = jnp.max(v.reshape(HALF // 16, 16, HALF), axis=0)
                    top = v if top is None else jnp.maximum(top, v)
                top = jnp.max(top.astype(F32), axis=0, keepdims=True) * SCALE
                total = None
                for k in range(KK):
                    for j in range(0, HALF, SLAB):
                        v = (wide[k][j:j + SLAB] - top) - c2_t[r, k, h * HALF + j:h * HALF + j + SLAB, i:i + HALF]
                        p = jnp.sum(jnp.exp2(v).reshape(SLAB // 8, 8, HALF), axis=0)
                        total = p if total is None else total + p
                m2[h, g, q:q + 1, i:i + HALF] = top
                s2[h, g, q:q + 1, i:i + HALF] = jnp.sum(total, axis=0, keepdims=True)

    def both_halves(g):
        top = jnp.maximum(m2[0, g], m2[1, g])
        total = s2[0, g] * jnp.exp2(m2[0, g] - top) + s2[1, g] * jnp.exp2(m2[1, g] - top)
        return top + jnp.log2(total)

    def take_chunk(step, g):
        landed(a_recv.at[step, g], NCOL - 1, a_rs.at[step, g])
        source = slm[g] - lse2(a_recv[step, g])
        if step == ITERS - 1:
            spot[g] = source * UNSCALE
        st[g] = jnp.concatenate([source, jnp.zeros_like(source)], axis=0).T

    def target_part(g, halves):
        for q in range(CHUNK):
            r = g * CHUNK + q
            wide = jnp.broadcast_to(st[g, :, q:q + 1], (BS, HALF))
            wide_b = (wide * UNSCALE).astype(BF16)
            for k in range(KK):
                for h in halves:
                    js = slice(h * HALF, (h + 1) * HALF)
                    v = wide_b - cost[r, k, :, js]
                    v = jnp.max(v.reshape(BS // 16, 16, HALF), axis=0)
                    top = jnp.max(v.astype(F32), axis=0, keepdims=True) * SCALE
                    total = None
                    for i in range(0, BS, SLAB):
                        v = (wide[i:i + SLAB] - top) - c2[r, k, i:i + SLAB, js]
                        p = jnp.sum(jnp.exp2(v).reshape(SLAB // 8, 8, HALF), axis=0)
                        total = p if total is None else total + p
                    j = q * KK + k
                    ment[h, g, j:j + 1, :] = top
                    sent[h, g, j:j + 1, :] = jnp.sum(total, axis=0, keepdims=True)

    def scatter(step, h):
        entries = (ment[h] + jnp.log2(sent[h])).reshape(ENT, HALF)
        blocks = named[...]
        peak = jnp.full((ENT, HALF), LOWEST, F32)
        for e in range(ENT):
            peak = jnp.maximum(peak, jnp.where(blocks == cand(e), entries[e:e + 1], LOWEST))
        shares = jnp.exp2(entries - peak)
        mass = jnp.zeros((ENT, HALF), F32)
        for e in range(ENT):
            mass = mass + jnp.where(blocks == cand(e), shares[e:e + 1], 0.0)
        merged = peak + jnp.log2(mass)
        first = merged.astype(BF16)
        rest = merged - first.astype(F32)
        second = rest.astype(BF16)
        third = (rest - second.astype(F32)).astype(BF16)
        pieces = jnp.concatenate([first, second, third, jnp.zeros_like(third)], axis=0)
        spread = jnp.dot(onehot[...], pieces, preferred_element_type=F32) + missing[...]
        dense[step, h] = spread.reshape(PLANE, 8, HALF)
        r_recv[step, h, me] = dense[step, h, me]

        for s in FAR_PLANE:
            peer, index = plane_peer(s)
            pltpu.make_async_remote_copy(
                src_ref=dense.at[step, h, index], dst_ref=r_recv.at[step, h, me],
                send_sem=r_ss.at[step, h], recv_sem=r_rs.at[step, h],
                device_id=peer, device_id_type=MESH,
            ).start()

    def along_z(step, h):
        landed(r_recv.at[step, h], PLANE - 1, r_rs.at[step, h])
        part = lse2(r_recv[step, h])
        z_src[step, h] = part
        z_recv[step, h, z] = part

        for s in FAR_Z:
            pltpu.make_async_remote_copy(
                src_ref=z_src.at[step, h], dst_ref=z_recv.at[step, h, z],
                send_sem=z_ss.at[step, h], recv_sem=z_rs.at[step, h],
                device_id=z_peer(s), device_id_type=MESH,
            ).start()

    def own_copy(h):
        return pltpu.make_async_copy(t_src.at[ITERS - 1, h], tgt_out.at[h, me], out_sem.at[h])

    def source_copy():
        return pltpu.make_async_copy(held, src_out, out_sem.at[2])

    def spread_target(step, h):
        landed(z_recv.at[step, h], NZ - 1, z_rs.at[step, h])
        target = tlm[:, h * HALF:(h + 1) * HALF] * LOG2E - lse2(z_recv[step, h])
        if step < ITERS - 1:
            t_src[step, h] = target
            t_recv[step][h][me] = target
        else:
            t_src[step, h] = target * UNSCALE
            own_copy(h).start()

        for s in FAR_PLANE:
            pltpu.make_async_remote_copy(
                src_ref=t_src.at[step, h], dst_ref=t_recv[step][h].at[me],
                send_sem=t_ss.at[step, h], recv_sem=t_rs.at[step, h],
                device_id=plane_peer(s)[0], device_id_type=MESH,
            ).start()

    for step in range(ITERS):
        if step > 0:
            for h in range(2):
                landed(t_recv[step - 1][h], PLANE - 1, t_rs.at[step - 1, h])
                gather(step, h)

                def source_rows(g, _):
                    if h == 0:
                        source_half(2 * g, h)
                        source_half(2 * g + 1, h)
                    else:
                        source_half(g, h)
                        keep_chunk(step, g, both_halves(g))
                        send_chunk(step, g)
                    return 0

                lax.fori_loop(0, CHUNKS if h else CHUNKS // 2, source_rows, 0)

        def target_rows_first(g, _):
            take_chunk(step, g + 1)
            target_part(g, (0,))
            return 0

        def target_rows_second(g, _):
            target_part(2 * g, (1,))
            target_part(2 * g + 1, (1,))
            return 0

        take_chunk(step, 0)
        lax.fori_loop(0, CHUNKS - 1, target_rows_first, 0)
        target_part(CHUNKS - 1, (0,))
        scatter(step, 0)
        lax.fori_loop(0, CHUNKS // 2, target_rows_second, 0)
        scatter(step, 1)
        if step == 0:
            tlm_copy().wait()
            lax.fori_loop(0, ROWS, scale_turned, 0)
        if step == ITERS - 1:
            for g in range(CHUNKS):
                held[g * CHUNK:(g + 1) * CHUNK] = spot[g]
            source_copy().start()
        along_z(step, 0)
        along_z(step, 1)
        spread_target(step, 0)
        spread_target(step, 1)

    for h in range(2):
        landed(t_recv[ITERS - 1][h], PLANE - 1, t_rs.at[ITERS - 1, h])
        own_copy(h).wait()
    source_copy().wait()

    for step in range(ITERS):
        ref = a_recv.at[step, :, pl.ds(0, NCOL - 1)]
        pltpu.make_async_copy(ref, ref, a_ss.at[step]).wait()
        for h in range(2):
            landed(r_recv.at[step, h], PLANE - 1, r_ss.at[step, h])
            landed(z_recv.at[step, h], NZ - 1, z_ss.at[step, h])
            landed(t_recv[step][h], PLANE - 1, t_ss.at[step, h])


def hand_over(source, target, src_out, tgt_out, held_s, held_t, in_sem, out_sem):
    ways = [(source, held_s, src_out)]
    size = tgt_out.shape[0] * 2 // PIECES
    for i in range(PIECES):
        h, first = i % 2, i // 2 * size
        part = pl.ds(first, size)
        ways.append((
            target.at[h, part], held_t.at[h, part], tgt_out.at[part, pl.ds(h * HALF, HALF)]
        ))
    ins = [pltpu.make_async_copy(a, v, in_sem.at[i]) for i, (a, v, _) in enumerate(ways)]
    outs = [pltpu.make_async_copy(v, b, out_sem.at[i]) for i, (_, v, b) in enumerate(ways)]
    for c in ins:
        c.start()
    for c, d in zip(ins, outs):
        c.wait()
        d.start()
    for d in outs:
        d.wait()


def per_device(block_cost, candidates, source_logmass, target_logmass):
    vmem = pl.BlockSpec(memory_space=pltpu.VMEM)
    hbm = pl.BlockSpec(memory_space=pl.ANY)
    dma = pltpu.SemaphoreType.DMA
    scratch = [
        ((ROWS, KK, BS, BS), BF16),
        ((ROWS, KK, BS, BS), F32),
        ((ROWS, KK, BS, BS), BF16),
        ((ROWS, KK, BS, BS), F32),
        ((8, BS), F32),
        ((CHUNKS, CHUNK, BS), F32),
        ((CHUNKS, CHUNK, BS), F32),
        ((ROWS, BS), F32),
        ((CHUNKS, BS, 8), F32),
        ((ENT // 8, 8, HALF), F32),
        ((2, CHUNKS, HALF, 8), F32),
        ((2, CHUNKS, CHUNK, BS), F32),
        ((2, CHUNKS, CHUNK, BS), F32),
        ((2, ENT // 8, 8, HALF), F32),
        ((2, ENT // 8, 8, HALF), F32),
        ((ENT, HALF), jnp.int32),
        ((BS, HALF), BF16),
        ((BS, HALF), F32),
        ((ITERS, CHUNKS, CHUNK, BS), F32),
        ((ITERS, CHUNKS, NCOL, CHUNK, BS), F32),
        ((ITERS, 2, PLANE, 8, HALF), F32),
        ((ITERS, 2, PLANE, 8, HALF), F32),
        ((ITERS, 2, 8, HALF), F32),
        ((ITERS, 2, NZ, 8, HALF), F32),
        ((ITERS, 2, 8, HALF), F32),
    ] + [((PLANE, 8, HALF), F32)] * 2
    source, target = pl.pallas_call(
        body,
        name="sinkhorn",
        out_shape=(
            jax.ShapeDtypeStruct(source_logmass.shape, F32),
            jax.ShapeDtypeStruct((2, PLANE, 8, HALF), F32),
        ),
        in_specs=[pl.BlockSpec(memory_space=pltpu.SMEM), hbm, vmem, hbm],
        out_specs=(hbm, hbm),
        scratch_shapes=[pltpu.VMEM(*s) for s in scratch]
        + [dma((ROWS + 1,)), dma((3,)), dma((ITERS,)), dma((ITERS, CHUNKS))]
        + [dma((ITERS, 2))] * 6,
        compiler_params=pltpu.CompilerParams(
            collective_id=0, has_side_effects=True, vmem_limit_bytes=60 << 20
        ),
    )(candidates.T, block_cost, source_logmass, target_logmass)
    return pl.pallas_call(
        hand_over,
        name="hand_over",
        out_shape=(
            jax.ShapeDtypeStruct(source_logmass.shape, F32),
            jax.ShapeDtypeStruct(target_logmass.shape, F32),
        ),
        in_specs=[hbm, hbm],
        out_specs=(hbm, hbm),
        scratch_shapes=[
            pltpu.VMEM(source_logmass.shape, F32),
            pltpu.VMEM((2, PLANE * 8, HALF), F32),
            dma((PIECES + 1,)),
            dma((PIECES + 1,)),
        ],
    )(source, target.reshape(2, PLANE * 8, HALF))


def solution(mesh):
    return jax.shard_map(
        per_device,
        mesh=mesh,
        in_specs=(P("row", "col", None, None), P("row", "col"), P("row", None), P()),
        out_specs=(P("row", None), P()),
        check_vma=False,
    )
```
